1024 devices in a mesh: ty: 16 (over y, core), tx: 32 (over x_lo, z), grp: 2 (over x_hi).
Axes of the slice: x: 4 (x_hi: 2, x_lo: 2; x = x_hi * 2 + x_lo), y: 8, z: 16, core: 2. Of those that a mesh axis runs over, the one named last changes fastest.
Arguments:
- innovation: float32 [2, 131072, 2, 128], P(None, ('ty', 'tx', 'grp')), may hold values from -6 to 6
- obs_weight: float32 [2, 131072, 128], P(None, ('ty', 'tx', 'grp')), may hold values from 0.2 to 1
- depth_level: int32 [2, 131072, 128], P(None, ('ty', 'tx', 'grp')), may hold values from 0 to 7
- target_tile: int32 [2, 131072, 1], P(None, ('ty', 'tx', 'grp')), may hold values from 0 to 31; in each aligned block of 128 rows (0 to 127, 128 to 255, ..., all dimensions but the last counted through in order) at most 16 rows name the same one
- target_cell: int32 [2, 131072], P(None, ('ty', 'tx', 'grp')), may hold values from 0 to 1023
- land_sea: int32 [128, 8192], P('ty', ('tx', 'grp')), may hold values from 0 to 1, as said below
- horiz_diff: float32 [128, 8192], P('ty', ('tx', 'grp')), may hold values from 0.05 to 0.2
- vert_diff: float32 [8, 128, 8192], P(None, 'ty', ('tx', 'grp')), may hold values from 0.01 to 0.1
- coupling: float32 [5, 5], replicated, may hold values from -0.4 to 0.4
- ice_sensitivity: float32 [2, 4, 128, 8192], P(None, None, ('ty', 'grp'), 'tx'), may hold values from -6 to 6
Outputs:
- adjoint_state: float32 [5, 8, 128, 8192], P(None, None, 'ty', ('tx', 'grp'))
The draws below stay inside these ranges and needn't reach their ends.
Inputs may be any that keep to these rules, and one draw needn't show every extreme that they name: `target_tile`: the rows of one device in one window name one tile column at most 16 times, and some device names one exactly 16 times. `target_cell`: cell index within the tile, row-major over 8 x 128. `land_sea`: 1 marks ocean, 0 land; the first and last grid rows are land.
All inputs are finite; a program needn't handle non-finite values.
Results may differ from the reference program's by a relative error of at most 0.00013.
Values sent between devices are 32-bit elements; how exact they have to be, the bound alone decides.
A program may use at most 32 MiB of HBM per device.

```python
import math
import jax
import jax.numpy as jnp
import numpy as np
from jax import lax

F = 5
VARS = 2
ICEV = 4
DEPTH = 128
LEV = 8
CY = 8
CX = 128
P_DEV = 128
ITERS = 2
SUB = 2
NY = 128
NX = 8192
NPROF = 131072
CAP = 16
N_TX = 32
N_GRP = 2


def draw_land_sea(key, part):
    key = jax.random.fold_in(key, 11)
    coin_toss = jax.random.randint(key, (NY, NX), 0, 10)
    ocean_cells = (coin_toss < 7).astype(jnp.int32)
    row_index = jnp.arange(NY, dtype=jnp.int32)[:, None]
    polar_rows = jnp.logical_or(row_index == 0, row_index == NY - 1)
    return jnp.where(polar_rows, 0, ocean_cells).astype(jnp.int32)


def place_ends(result, stream_key, least, high):
    longest = result.shape.index(max(result.shape))
    spots = []
    for shift in (0, 1):
        where = [jax.random.randint(jax.random.fold_in(stream_key, axis), (), 0, length) for axis, length in enumerate(result.shape)]
        where[longest] = (where[longest] + shift) % result.shape[longest]
        spots.append(tuple(where))
    return result.at[spots[0]].set(least).at[spots[1]].set(high)


def block_levels(own_key, extent, pieces, smallest, largest):
    factor_of = 1.0
    for position, shards_of in pieces:
        draws = jax.random.uniform(jax.random.fold_in(jax.random.fold_in(own_key, 6), position), (shards_of,), jnp.float32, smallest / len(pieces), largest / len(pieces))
        factor_of = factor_of * jnp.repeat(jnp.exp(draws), extent[position] // shards_of).reshape((-1,) + (1,) * (len(extent) - 1 - position))
    return factor_of


def routed_block(rng, own, number, rows, number_of, top, reach, slope):
    order = jax.random.permutation(rng, number_of)
    heavy_load, common = portions_of(number_of, rows * top, reach, slope, True), portions_of(number_of, rows * top, reach, slope, False)
    places = jnp.arange(number_of)

    def named(sizes, turn):
        used = int((sizes > 0).sum())
        fixed = max(1, used // 4)
        shifted = fixed + (places - fixed + turn * (used - fixed)) % max(1, number_of - fixed)
        return jnp.zeros((number_of,), jnp.int32).at[order[jnp.where(places < fixed, places, shifted)]].set(jnp.asarray(sizes, jnp.int32))

    sizes = jnp.where(number % 4 == 0, named(heavy_load, number // 4), named(common, number - number // 4 - 1))
    mixed = jax.random.permutation(jax.random.fold_in(own, 3), number_of)
    giver, sink = mixed[0:number_of // 2 * 2:2], mixed[1:number_of // 2 * 2:2]
    margin = jnp.minimum(sizes[giver] - 1, reach - sizes[sink]) // 2
    margin = jnp.where((giver == order[0]) | (sink == order[0]) | (sizes[sink] == 0), 0, jnp.maximum(margin, 0))
    shifted = jax.random.randint(jax.random.fold_in(own, 4), (number_of // 2,), 0, 1 << 20) % (margin + 1)
    sizes = sizes.at[giver].add(-shifted).at[sink].add(shifted)
    labels = jnp.searchsorted(jnp.cumsum(sizes), jnp.arange(rows * top), side="right").astype(jnp.int32)
    listing = labels.reshape(top, rows).T
    listing = listing[jax.random.permutation(jax.random.fold_in(own, 1), rows)]
    turn = jax.random.randint(jax.random.fold_in(own, 2), (rows, 1), 0, top)
    return jnp.take_along_axis(listing, (jnp.arange(top)[None, :] + turn) % top, axis=1)


def portions_of(amount, total, most, lean, full):
    portions = [(1 << 20) // math.isqrt(rank ** lean) + 1 for rank in range(1, amount + 1)]
    largest = most if full else min(most, max(-(-total // amount), total * portions[0] // sum(portions)))
    least = 1 if total - largest >= amount - 1 else 0
    holding, rest = [largest] + [least] * (amount - 1), total - largest - least * (amount - 1)
    while rest > 0:
        candidates = [i for i in range(1, amount) if holding[i] < largest] or [i for i in range(1, amount) if holding[i] < most]
        whole, left = sum([portions[i] for i in candidates]), rest
        for i in candidates:
            more = min(most - holding[i], max(1, left * portions[i] // whole), rest)
            holding[i] = holding[i] + more
            rest = rest - more
    return np.array(holding)


def centred(key, extent, width, reach, shards=(), held_as=jnp.bfloat16):
    drawn = width * jax.random.normal(key, extent, jnp.float32)
    if shards:
        drawn = drawn * block_levels(key, extent, shards, -0.22, 0.18)
    return jnp.clip(drawn, -reach, reach).astype(held_as)


def setup_inputs(seed: int = 0) -> dict:
    arg_keys = jax.random.split(jax.random.key(seed), 11)
    innovation = centred(arg_keys[0], (ITERS, NPROF, VARS, DEPTH), 1.0, 6.0, ((1, 1024),), jnp.float32)
    obs_weight = jnp.clip(jnp.exp(math.log(1.0) - 1.609438 * jax.random.uniform(arg_keys[1], (ITERS, NPROF, DEPTH), jnp.float32) ** block_levels(arg_keys[1], (ITERS, NPROF, DEPTH), ((1, 1024),), -0.2, 0.2)), 0.2, 1.0)
    depth_level = place_ends(jax.random.randint(arg_keys[2], (ITERS, NPROF, DEPTH), 0, LEV), jax.random.fold_in(arg_keys[2], 1), 0, LEV - 1).astype(jnp.int32)
    target_tile_keys = jax.random.split(jax.random.fold_in(arg_keys[3], 1), ITERS * NPROF // P_DEV)
    target_tile_turns = jax.random.permutation(jax.random.fold_in(arg_keys[3], 3), ITERS * NPROF // P_DEV)
    target_tile = jax.vmap(lambda own, number: routed_block(jax.random.fold_in(arg_keys[3], 2), own, number, P_DEV, N_TX, 1, CAP, 2))(target_tile_keys, target_tile_turns).reshape((ITERS, NPROF, 1))
    target_cell = place_ends(jax.random.randint(arg_keys[4], (ITERS, NPROF), 0, CY * CX), jax.random.fold_in(arg_keys[4], 1), 0, (CY * CX) - 1).astype(jnp.int32)
    land_sea = draw_land_sea(jax.random.fold_in(arg_keys[10], 71), 0)
    horiz_diff = jnp.clip(jnp.exp(math.log(0.2) - 1.3862944 * jax.random.uniform(arg_keys[6], (NY, NX), jnp.float32) ** block_levels(arg_keys[6], (NY, NX), ((0, 16), (1, 64)), -0.2, 0.2)), 0.05, 0.2)
    vert_diff = jnp.clip(jnp.exp(math.log(0.1) - 2.3025851 * jax.random.uniform(arg_keys[7], (LEV, NY, NX), jnp.float32) ** block_levels(arg_keys[7], (LEV, NY, NX), ((1, 16), (2, 64)), -0.2, 0.2)), 0.01, 0.1)
    coupling = centred(arg_keys[8], (F, F), 0.1, 0.4, (), jnp.float32)
    ice_sensitivity = centred(arg_keys[9], (ITERS, ICEV, NY, NX), 1.0, 6.0, ((2, 32), (3, 32)), jnp.float32)
    return {"innovation": innovation, "obs_weight": obs_weight, "depth_level": depth_level, "target_tile": target_tile, "target_cell": target_cell, "land_sea": land_sea, "horiz_diff": horiz_diff, "vert_diff": vert_diff, "coupling": coupling, "ice_sensitivity": ice_sensitivity}


EXACT_DOT = lax.Precision.HIGHEST


def adjoint_step(current, horiz_diff, ocean_mask, vert_diff, coupling):
    lateral = jnp.zeros_like(current)
    for offset, roll_axis in ((-1, 2), (1, 2), (-1, 3), (1, 3)):
        near_state = jnp.roll(current, offset, roll_axis)
        near_diff = jnp.roll(horiz_diff, offset, roll_axis - 2)
        near_ocean = jnp.roll(ocean_mask, offset, roll_axis - 2)
        weight = 0.5 * (horiz_diff + near_diff) * ocean_mask * near_ocean
        lateral = lateral + weight * (near_state - current)
    upper = vert_diff[:-1] * (current[:, 1:] - current[:, :-1])
    bottom = -vert_diff[-1:] * current[:, -1:]
    vertical_flux = jnp.concatenate([upper, bottom], axis=1)
    below = jnp.concatenate([jnp.zeros_like(vertical_flux[:, :1]), vertical_flux[:, :-1]], axis=1)
    diffused = current + lateral + (vertical_flux - below)
    coupled = diffused + jnp.einsum('gf,glyx->flyx', coupling, diffused, precision=EXACT_DOT)
    return ocean_mask * coupled


def reference(innovation, obs_weight, depth_level, target_tile, target_cell, land_sea, horiz_diff, vert_diff, coupling, ice_sensitivity):
    ocean_mask = land_sea.astype(jnp.float32)
    profile_count = innovation.shape[1]
    row_ids = jnp.arange(profile_count, dtype=jnp.int32)
    source = row_ids // P_DEV
    tile_row = source // (N_TX * N_GRP)
    group_id = source % N_GRP
    var_ids = jnp.arange(VARS, dtype=jnp.int32)
    current = jnp.zeros((F, LEV, NY, NX), jnp.float32)
    for window in range(ITERS):
        weighted = obs_weight[window][:, None, :] * innovation[window]
        columns = jnp.zeros((profile_count, VARS, LEV), jnp.float32)
        columns = columns.at[row_ids[:, None, None], var_ids[None, :, None], depth_level[window][:, None, :]].add(weighted)
        cell_ids = target_cell[window]
        y_index = tile_row * CY + cell_ids // CX
        x_index = (target_tile[window][:, 0] * N_GRP + group_id) * CX + cell_ids % CX
        profile = jnp.zeros((VARS, LEV, NY, NX), jnp.float32)
        profile = profile.at[:, :, y_index, x_index].add(jnp.transpose(columns, (1, 2, 0)))
        forcing = jnp.zeros((F, LEV, NY, NX), jnp.float32)
        forcing = forcing.at[:VARS].add(profile)
        forcing = forcing.at[:ICEV, 0].add(ice_sensitivity[window])
        current = current + ocean_mask * forcing
        for substep in range(SUB):
            current = adjoint_step(current, horiz_diff, ocean_mask, vert_diff, coupling)
    return current
```

```python
import functools

import jax
import jax.numpy as jnp
from jax import lax
from jax.experimental import pallas as pl
from jax.experimental.pallas import tpu as pltpu
from jax.sharding import PartitionSpec as P

F = 5
LEV = 8
VARS = 2
ICEV = 4
ROWS = 8
LANES = 128
DEPTH = 128
PROFS = 128
ITERS = 2
SUB = 2
SLOTS = 32
N_FORCED = VARS * LEV + (ICEV - VARS)
N_STATIC = LEV + 2
MESH = pl.DeviceIdType.MESH
F32 = jnp.float32
BF16 = jnp.bfloat16
NT = (((1,), (1,)), ((), ()))

FORCED = [(f, l) for f in range(VARS) for l in range(LEV)] + [(f, 0) for f in range(VARS, ICEV)]

L_LEVEL, L_WEIGHT, L_INNOV = 0, 2, 4
L_TILE, L_CELL, L_LAND, L_HDIFF, L_VDIFF, L_ICE, L_OWN = 6, 7, 8, 9, 10, 11, 12
N_LOCAL = 14
R_ROUTE, R_ICE, R_STAT_Y, R_STAT_X, R_F_Y, R_F_X = 0, 2, 3, 4, 5, 7
N_REMOTE = 9


def iota(shape, axis):
    return lax.broadcasted_iota(jnp.int32, shape, axis)


def split(x):
    high = x.astype(BF16)
    low = (x - high.astype(F32)).astype(BF16)
    return high, low


def roll_lanes(x, shift):
    shift %= LANES
    return x if shift == 0 else pltpu.roll(x, shift, 1)


def dot_nt(a, b):
    return lax.dot_general(a, b, NT, preferred_element_type=F32)


def pack_messages(weight, level, innovs, tile, cell):
    level_t = level.T
    columns = []
    for innov in innovs:
        weighted_t = (weight * innov).T
        rows = [
            jnp.sum(jnp.where(level_t == l, weighted_t, 0.0), axis=0, keepdims=True) for l in range(LEV)
        ]
        columns.append(jnp.concatenate(rows, axis=0))
    named = tile == iota((SLOTS, PROFS), 0)
    named_f = named.astype(F32)
    named_b = named_f.astype(BF16)
    before = (iota((PROFS, PROFS), 0) < iota((PROFS, PROFS), 1)).astype(F32).astype(BF16)
    counts = lax.dot_general(named_b, before, (((1,), (0,)), ((), ())), preferred_element_type=F32)
    rank = jnp.sum(named_f * counts, axis=0, keepdims=True).astype(jnp.int32)
    cell_y = (cell // LANES).astype(F32)
    cell_x = (cell % LANES).astype(F32)
    high, low = [], []
    parts = []
    for column in columns:
        top = column.astype(BF16).astype(F32)
        parts.append((top, column - top))
    for upper in range(2):
        for top, rest in parts:
            for r in range(8):
                here = rank == upper * 8 + r
                high.append(jnp.where(here, top, 0.0))
                low.append(jnp.where(here, rest, 0.0))
    row = iota((8, PROFS), 0)
    zero = jnp.zeros((8, PROFS), F32)
    for r in range(8):
        first, second = rank == r, rank == r + 8
        block = jnp.where(jnp.logical_and(row == 0, first), cell_y, 0.0)
        block = jnp.where(jnp.logical_and(row == 1, first), cell_x, block)
        block = jnp.where(jnp.logical_and(row == 2, second), cell_y, block)
        block = jnp.where(jnp.logical_and(row == 3, second), cell_x, block)
        high.append(block)
        low.append(zero)
    high += [zero] * 8
    low += [zero] * 8
    values = jnp.concatenate(
        [jnp.concatenate(high, axis=0).astype(BF16), jnp.concatenate(low, axis=0).astype(BF16)], axis=1
    )
    return dot_nt(jnp.concatenate([named_b, named_b], axis=1), values)


def gather_cells(first, second, cells):
    got = jnp.concatenate([first, second, roll_lanes(first, -8), roll_lanes(second, -8)], axis=0).T
    where_ = jnp.concatenate(
        [cells, roll_lanes(cells, -2), roll_lanes(cells, -8), roll_lanes(cells, -10)], axis=0
    ).T
    top = got.astype(BF16).astype(F32)
    rest = got - top
    y_of_row = iota((ROWS, LANES), 0).astype(F32)
    x_of_row = iota((LANES, LANES), 0).astype(F32)
    left, right = [], []
    for r in range(0, 8, 2):
        y_here = where_[r * 8 : r * 8 + 1] == y_of_row
        x_here = (where_[r * 8 + 1 : r * 8 + 2] == x_of_row).astype(F32).astype(BF16)
        for part in (top, rest):
            blocks = []
            for v in range(VARS):
                for l in range(LEV):
                    at = v * 64 + r * 8 + l
                    blocks.append(jnp.where(y_here, part[at : at + 1], 0.0))
            left.append(jnp.concatenate(blocks, axis=0).astype(BF16))
            right.append(x_here)
    return dot_nt(jnp.concatenate(left, axis=1), jnp.concatenate(right, axis=1))


def pack_edges(items):
    lane = iota((ROWS, LANES), 1)
    last = jnp.zeros((ROWS, LANES), F32)
    first = jnp.zeros((ROWS, LANES), F32)
    for slot, level, rows in items:
        at = 16 * level + 4 * slot
        turned = roll_lanes(rows, at + 4)
        last = jnp.where(jnp.logical_and(lane >= at, lane < at + 4), turned, last)
        first = jnp.where(jnp.logical_and(lane >= at + 4, lane < at + 8), turned, first)
    return last, first


def strip(slot, from_left, own_last, own_first, from_right):
    group = iota((ROWS, LANES), 1) % 16
    low = jnp.where(group < 4, roll_lanes(from_left, -4 * slot), roll_lanes(own_first, -4 * slot))
    high = jnp.where(group < 12, roll_lanes(own_last, 8 - 4 * slot), roll_lanes(from_right, 8 - 4 * slot))
    return jnp.where(group < 8, low, high)


def strips(slots, received, own):
    upper = iota((ROWS, LANES), 0) < 4
    left_halo = jnp.where(upper, received[1], received[2])
    right_halo = jnp.where(upper, received[4], received[5])
    sides = ((received[0], received[3]), (left_halo, right_halo))
    return [
        tuple(strip(slot, sides[t][0], own[t][0], own[t][1], sides[t][1]) for t in range(2)) for slot in slots
    ]


def y_neighbours(pair):
    row = iota((ROWS, LANES), 0)
    a, b = pair
    next_a, next_b = pltpu.roll(a, ROWS - 1, 0), pltpu.roll(b, ROWS - 1, 0)
    prev_a, prev_b = pltpu.roll(a, 1, 0), pltpu.roll(b, 1, 0)
    plus = (jnp.where(row == ROWS - 1, next_b, next_a), jnp.where(row == ROWS - 1, next_a, next_b))
    minus = (jnp.where(row == 0, prev_b, prev_a), jnp.where(row == 0, prev_a, prev_b))
    return plus, minus


def edge_pair(one):
    group = iota((ROWS, LANES), 1) % 16
    return jnp.where(group == 13, roll_lanes(one, 10), one)


def x_neighbours(one, edges, level):
    lane = iota((ROWS, LANES), 1)
    halo = roll_lanes(edges, LANES - 1 - 12 - 16 * level)
    plus = jnp.where(lane == LANES - 1, halo, roll_lanes(one, -1))
    minus = jnp.where(lane == 0, halo, roll_lanes(one, 1))
    return plus, minus


def strip_x_neighbours(one):
    return roll_lanes(one, -1), roll_lanes(one, 1)


def weights_of(diff, ocean, x_pairs):
    (diff_n, ocean_n) = (y_neighbours(diff), y_neighbours(ocean))
    out = []
    for t in range(2):
        near = [(diff_n[0][t], ocean_n[0][t]), (diff_n[1][t], ocean_n[1][t])] + list(x_pairs[t])
        faces = [0.5 * (diff[t] + d) * ocean[t] * o for d, o in near]
        out.append((1.0 - (faces[0] + faces[1] + faces[2] + faces[3]), faces))
    return out


def lateral(one, near, weights):
    centre, faces = weights
    total = centre * one
    for face, value in zip(faces, near):
        total = total + face * value
    return total


def couple(diffused, coef, ocean):
    out = []
    for f in range(F):
        total = None
        for g in range(F):
            if diffused[g] is not None:
                term = coef[g][f] * diffused[g]
                total = term if total is None else total + term
        out.append(ocean * total)
    return out


def step_strips(old, weights, vertical, ocean, coef):
    lane = iota((ROWS, LANES), 1)
    diffused = [[None] * F, [None] * F]
    for f in range(F):
        if old[f] is None:
            continue
        plus, minus = y_neighbours(old[f])
        for t in range(2):
            one = old[f][t]
            x_plus, x_minus = strip_x_neighbours(one)
            below = jnp.where(lane < LANES - 16, roll_lanes(one, -16), 0.0)
            flux = vertical[t] * (below - one)
            above = jnp.where(lane < 16, 0.0, roll_lanes(flux, 16))
            diffused[t][f] = lateral(one, (plus[t], minus[t], x_plus, x_minus), weights[t]) + (flux - above)
    coupled = [couple(diffused[t], coef, ocean[t]) for t in range(2)]
    return [(coupled[0][f], coupled[1][f]) for f in range(F)]


def step_tile(read, write, live, edges, weights, vertical, ocean, coef, tiles):
    above = [[None] * F, [None] * F]
    for l in range(LEV):
        diffused = [[None] * F, [None] * F]
        for f in range(F):
            here = read(f, l) if (f, l) in live else None
            below = read(f, l + 1) if (f, l + 1) in live else None
            near = y_neighbours(here) if here is not None else None
            for t in range(tiles):
                flux = None
                if here is not None and below is not None:
                    flux = vertical(l, t) * (below[t] - here[t])
                elif here is not None:
                    flux = -(vertical(l, t) * here[t])
                elif below is not None:
                    flux = vertical(l, t) * below[t]
                total = None
                if here is not None:
                    x_plus, x_minus = x_neighbours(here[t], edges[f][t], l)
                    total = lateral(here[t], (near[0][t], near[1][t], x_plus, x_minus), weights[t])
                if flux is not None:
                    total = flux if total is None else total + flux
                if above[t][f] is not None:
                    total = -above[t][f] if total is None else total - above[t][f]
                above[t][f] = flux
                diffused[t][f] = total
        for t in range(tiles):
            for f, value in enumerate(couple(diffused[t], coef, ocean[t])):
                write(f, l, t, value)


def kernel(
    sizes,
    innov,
    weight,
    level,
    tile,
    cell,
    land,
    hdiff,
    vdiff,
    coupling,
    ice,
    out,
    innov_v,
    weight_v,
    level_v,
    tile_v,
    cell_v,
    land_v,
    ice_v,
    stat,
    stat_y,
    stat_e,
    stat_x,
    send,
    recv,
    forced,
    forced_y,
    forced_e,
    forced_x,
    state,
    local_sem,
    send_sem,
    recv_sem,
):
    n_ty, n_tx, n_grp = sizes
    ty, tx, grp = lax.axis_index("ty"), lax.axis_index("tx"), lax.axis_index("grp")
    blocks = n_tx * n_grp
    block = tx * n_grp + grp
    right, left = (block + 1) % blocks, (block + blocks - 1) % blocks
    down, up = (ty + 1) % n_ty, (ty + n_ty - 1) % n_ty

    def at(row, column):
        return (row, column // n_grp, column % n_grp)

    partner = (ty, tx, 1 - grp)

    def fetch(src, dst, sem):
        copy = pltpu.make_async_copy(src, dst, local_sem.at[sem])
        copy.start()
        return copy

    def put(src, dst, sem, device):
        pltpu.make_async_remote_copy(
            src_ref=src,
            dst_ref=dst,
            send_sem=send_sem.at[sem],
            recv_sem=recv_sem.at[sem],
            device_id=device,
            device_id_type=MESH,
        ).start()

    def wait(ref, sems, sem):
        pltpu.make_async_copy(ref, ref, sems.at[sem]).wait()

    profile_rows = PROFS * VARS
    loads = []
    for w in range(ITERS):
        loads.append(
            [
                fetch(level.at[w], level_v.at[w], L_LEVEL + w),
                fetch(weight.at[w], weight_v.at[w], L_WEIGHT + w),
                fetch(
                    innov.at[pl.ds(w * profile_rows, profile_rows)],
                    innov_v.at[pl.ds(w * profile_rows, profile_rows)],
                    L_INNOV + w,
                ),
            ]
        )
        if w == 0:
            loads[0] += [fetch(tile, tile_v, L_TILE), fetch(cell, cell_v, L_CELL)]
    ice_here = ice.at[:, :, :, pl.ds(pl.multiple_of(grp * LANES, LANES), LANES)]
    ice_there = ice.at[:, :, :, pl.ds(pl.multiple_of((1 - grp) * LANES, LANES), LANES)]
    static_loads = [
        fetch(land, land_v, L_LAND),
        fetch(hdiff, stat.at[LEV], L_HDIFF),
        fetch(vdiff, stat.at[pl.ds(0, LEV)], L_VDIFF),
        fetch(ice_here, ice_v.at[grp], L_ICE),
    ]

    barrier = pltpu.get_barrier_semaphore()
    around = [(r, c) for c in (right, left) for r in (ty, down, up)] + [(down, block), (up, block)]
    for r, c in around:
        pl.semaphore_signal(barrier, inc=1, device_id=at(r, c), device_id_type=MESH)

    def greet(k, carry):
        pl.semaphore_signal(barrier, inc=1, device_id=(ty, (tx + k) % n_tx, grp), device_id_type=MESH)
        return carry

    lax.fori_loop(1, n_tx, greet, 0)

    def route(w):
        for load in loads[w]:
            load.wait()
        innovs = [innov_v[pl.ds(w * profile_rows + v, PROFS, stride=VARS), :] for v in range(VARS)]
        messages = pack_messages(
            weight_v[w], level_v[w], innovs, tile_v[pl.ds(w, 1), :], cell_v[pl.ds(w, 1), :]
        )
        for j in range(3):
            send[w, :, j, :] = messages[:, j * LANES : (j + 1) * LANES]
        if w == 0:
            pl.semaphore_wait(barrier, n_tx - 1 + len(around))
        own = fetch(send.at[w, tx], recv.at[w, tx], L_OWN + w)

        def to_peer(k, carry):
            peer = (tx + k) % n_tx
            put(send.at[w, peer], recv.at[w, tx], R_ROUTE + w, (ty, peer, grp))
            return carry

        lax.fori_loop(1, n_tx, to_peer, 0)
        return own

    def exchange(rows, rows_y, edges, edges_x, sem_y, sem_x):
        put(rows.at[:, pl.ds(0, 4)], rows_y.at[:, pl.ds(0, 4)], sem_y, at(up, block))
        put(rows.at[:, pl.ds(4, 4)], rows_y.at[:, pl.ds(4, 4)], sem_y, at(down, block))
        for side, column in enumerate((right, left)):
            for slot, r in enumerate((ty, up, down)):
                put(edges.at[side], edges_x.at[side * 3 + slot], sem_x, at(r, column))

    if n_tx < SLOTS:
        recv[...] = jnp.zeros(recv.shape, F32)
    owns = [route(0)]
    put(ice_there, ice_v.at[grp], R_ICE, partner)
    for load in static_loads:
        load.wait()
    ocean_tile = land_v[...].astype(F32)
    stat[LEV + 1] = ocean_tile

    def static_items(ref):
        items = [(0, l, ref[l]) for l in range(LEV)]
        return items + [(1 + j, l, ref[LEV + j]) for j in range(2) for l in range(LEV)]

    last, first = pack_edges(static_items(stat))
    stat_e[0] = last
    stat_e[1] = first
    exchange(stat, stat_y, stat_e, stat_x, R_STAT_Y, R_STAT_X)
    owns.append(route(1))

    def force(w):
        owns[w].wait()
        wait(recv.at[w, pl.ds(0, n_tx - 1)], recv_sem, R_ROUTE + w)
        sums = gather_cells(recv[w, :, 0, :], recv[w, :, 1, :], recv[w, :, 2, :])
        if w == 0:
            wait(ice_v.at[0], recv_sem, R_ICE)
        items = []
        for i, (f, l) in enumerate(FORCED):
            value = sums[i * ROWS : (i + 1) * ROWS] if f < VARS else None
            if l == 0:
                melt = jnp.concatenate([ice_v[0, w, f], ice_v[1, w, f]], axis=0)
                value = melt if value is None else value + melt
            value = ocean_tile * value
            forced[w, i] = value
            items.append((f, l, value))
        last, first = pack_edges(items)
        forced_e[w, 0] = last
        forced_e[w, 1] = first
        exchange(
            forced.at[w], forced_y.at[w], forced_e.at[w], forced_x.at[w], R_F_Y + w, R_F_X + w
        )

    force(0)
    force(1)

    wait(stat_y, recv_sem, R_STAT_Y)
    wait(stat_x, recv_sem, R_STAT_X)
    own_edges = ((stat_e[0], stat_e[1]), pack_edges(static_items(stat_y)))
    vertical_s, diff_s, ocean_s = strips((0, 1, 2), [stat_x[i] for i in range(6)], own_edges)
    diff = (stat[LEV], stat_y[LEV])
    ocean = (stat[LEV + 1], stat_y[LEV + 1])
    x_pairs, x_pairs_s = [], []
    for t in range(2):
        d = x_neighbours(diff[t], edge_pair(diff_s[t]), 0)
        o = x_neighbours(ocean[t], edge_pair(ocean_s[t]), 0)
        x_pairs.append(((d[0], o[0]), (d[1], o[1])))
        d, o = strip_x_neighbours(diff_s[t]), strip_x_neighbours(ocean_s[t])
        x_pairs_s.append(((d[0], o[0]), (d[1], o[1])))
    weights = weights_of(diff, ocean, x_pairs)
    weights_s = weights_of(diff_s, ocean_s, x_pairs_s)
    coef = [[coupling[g, f] + (1.0 if f == g else 0.0) for f in range(F)] for g in range(F)]

    def vertical(l, t):
        return stat[l] if t == 0 else stat_y[l]

    def forced_strips(w):
        wait(forced_y.at[w], recv_sem, R_F_Y + w)
        wait(forced_x.at[w], recv_sem, R_F_X + w)
        halo_items = [(f, l, forced_y[w, i]) for i, (f, l) in enumerate(FORCED)]
        own_edges = ((forced_e[w, 0], forced_e[w, 1]), pack_edges(halo_items))
        return strips(range(ICEV), [forced_x[w, i] for i in range(6)], own_edges)

    index = {item: i for i, item in enumerate(FORCED)}
    whole = {(f, l) for f in range(F) for l in range(LEV)}
    packed = forced_strips(0) + [None]

    def read_forced(f, l):
        return forced[0, index[f, l]], forced_y[0, index[f, l]]

    def reader(slot):
        return lambda f, l: (state[slot, 0, f * LEV + l], state[slot, 1, f * LEV + l])

    def writer(slot):
        def write(f, l, t, value):
            state[slot, t, f * LEV + l] = value

        return write

    def write_out(f, l, t, value):
        out[f, l] = value

    n_steps = ITERS * SUB
    for step in range(n_steps):
        end = step == n_steps - 1
        edges = [None if p is None else (edge_pair(p[0]), edge_pair(p[1])) for p in packed]
        step_tile(
            read_forced if step == 0 else reader(step % 2),
            write_out if end else writer((step + 1) % 2),
            set(FORCED) if step == 0 else whole,
            edges,
            weights,
            vertical,
            ocean,
            coef,
            1 if end else 2,
        )
        if not end:
            packed = step_strips(packed, weights_s, vertical_s, ocean_s, coef)
        if step == SUB - 1:
            slot = (step + 1) % 2
            added = forced_strips(1)
            for f in range(ICEV):
                packed[f] = tuple(packed[f][t] + added[f][t] for t in range(2))
            for i, (f, l) in enumerate(FORCED):
                state[slot, 0, f * LEV + l] += forced[1, i]
                state[slot, 1, f * LEV + l] += forced_y[1, i]

    for w in range(ITERS):
        wait(send.at[w, pl.ds(0, n_tx - 1)], send_sem, R_ROUTE + w)
        wait(forced.at[w], send_sem, R_F_Y + w)
        wait(forced_x.at[w], send_sem, R_F_X + w)
    wait(ice_v.at[0], send_sem, R_ICE)
    wait(stat, send_sem, R_STAT_Y)
    wait(stat_x, send_sem, R_STAT_X)


def per_device(sizes, innov, weight, level, tile, cell, land, hdiff, vdiff, coupling, ice):
    scratch = [
        pltpu.VMEM((ITERS * PROFS * VARS, DEPTH), F32),
        pltpu.VMEM((ITERS, PROFS, DEPTH), F32),
        pltpu.VMEM((ITERS, PROFS, DEPTH), jnp.int32),
        pltpu.VMEM((ITERS, PROFS), jnp.int32),
        pltpu.VMEM((ITERS, PROFS), jnp.int32),
        pltpu.VMEM((ROWS, LANES), jnp.int32),
        pltpu.VMEM((2, ITERS, ICEV, 4, LANES), F32),
        pltpu.VMEM((N_STATIC, ROWS, LANES), F32),
        pltpu.VMEM((N_STATIC, ROWS, LANES), F32),
        pltpu.VMEM((2, ROWS, LANES), F32),
        pltpu.VMEM((6, ROWS, LANES), F32),
        pltpu.VMEM((ITERS, SLOTS, 3, LANES), F32),
        pltpu.VMEM((ITERS, SLOTS, 3, LANES), F32),
        pltpu.VMEM((ITERS, N_FORCED, ROWS, LANES), F32),
        pltpu.VMEM((ITERS, N_FORCED, ROWS, LANES), F32),
        pltpu.VMEM((ITERS, 2, ROWS, LANES), F32),
        pltpu.VMEM((ITERS, 6, ROWS, LANES), F32),
        pltpu.VMEM((2, 2, F * LEV, ROWS, LANES), F32),
        pltpu.SemaphoreType.DMA((N_LOCAL,)),
        pltpu.SemaphoreType.DMA((N_REMOTE,)),
        pltpu.SemaphoreType.DMA((N_REMOTE,)),
    ]
    anywhere = pl.BlockSpec(memory_space=pl.ANY)
    return pl.pallas_call(
        functools.partial(kernel, sizes),
        out_shape=jax.ShapeDtypeStruct((F, LEV, ROWS, LANES), F32),
        in_specs=[anywhere] * 8 + [pl.BlockSpec(memory_space=pltpu.SMEM), anywhere],
        out_specs=pl.BlockSpec(memory_space=pltpu.VMEM),
        scratch_shapes=scratch,
        compiler_params=pltpu.CompilerParams(
            collective_id=0, has_side_effects=True, vmem_limit_bytes=16 * 1024 * 1024
        ),
    )(
        innov.reshape(ITERS * PROFS * VARS, DEPTH),
        weight,
        level,
        tile.reshape(ITERS, PROFS),
        cell,
        land,
        hdiff,
        vdiff,
        coupling,
        ice,
    )


def solution(mesh):
    sizes = tuple(mesh.shape[axis] for axis in ("ty", "tx", "grp"))
    in_specs = (
        P(None, ("ty", "tx", "grp"), None, None),
        P(None, ("ty", "tx", "grp"), None),
        P(None, ("ty", "tx", "grp"), None),
        P(None, ("ty", "tx", "grp"), None),
        P(None, ("ty", "tx", "grp")),
        P("ty", ("tx", "grp")),
        P("ty", ("tx", "grp")),
        P(None, "ty", ("tx", "grp")),
        P(),
        P(None, None, ("ty", "grp"), "tx"),
    )
    out_specs = P(None, None, "ty", ("tx", "grp"))
    return jax.shard_map(
        functools.partial(per_device, sizes), mesh=mesh, in_specs=in_specs, out_specs=out_specs, check_vma=False
    )
```

```python
import functools

import jax
import jax.numpy as jnp
from jax import lax
from jax.experimental import pallas as pl
from jax.experimental.pallas import tpu as pltpu
from jax.sharding import PartitionSpec as P

F = 5
LEV = 8
VARS = 2
ICEV = 4
ROWS = 8
LANES = 128
DEPTH = 128
PROFS = 128
ITERS = 2
SUB = 2
SLOTS = 32
N_FORCED = VARS * LEV + (ICEV - VARS)
N_STATIC = LEV + 2
MESH = pl.DeviceIdType.MESH
F32 = jnp.float32
BF16 = jnp.bfloat16
NT = (((1,), (1,)), ((), ()))

FORCED = [(f, l) for f in range(VARS) for l in range(LEV)] + [(f, 0) for f in range(VARS, ICEV)]

L_LEVEL, L_WEIGHT, L_INNOV, L_TILE, L_CELL, L_LAND, L_HDIFF, L_VDIFF, L_ICE, L_COUPLING, L_OWN = range(11)
N_LOCAL = 11
R_ROUTE, R_ICE, R_STAT_Y, R_STAT_X, R_FORCED_Y, R_FORCED_RIGHT, R_FORCED_LEFT = range(7)
R_BORDER, R_BORDER_ICE, R_BORDER_LAND = range(7, 10)
N_REMOTE = 10

RANK_ROWS = 4
RANKS = 4
MESSAGE = RANK_ROWS + 1


def iota(shape, axis):
    return lax.broadcasted_iota(jnp.int32, shape, axis)


def split(x):
    high = x.astype(BF16)
    low = (x - high.astype(F32)).astype(BF16)
    return high, low


def roll_lanes(x, shift):
    shift %= LANES
    return x if shift == 0 else pltpu.roll(x, shift, 1)


def dot_nt(a, b):
    return lax.dot_general(a, b, NT, preferred_element_type=F32)


def level_sums(weight, level, innovs):
    level_t = level.T
    out = []
    for innov in innovs:
        weighted_t = (weight * innov).T
        rows = [
            jnp.sum(jnp.where(level_t == l, weighted_t, 0.0), axis=0, keepdims=True) for l in range(LEV)
        ]
        out.append(jnp.concatenate(rows, axis=0))
    return out


def rank_in_tile(tile):
    named = (tile == iota((SLOTS, PROFS), 0)).astype(F32)
    before = (iota((PROFS, PROFS), 0) < iota((PROFS, PROFS), 1)).astype(F32).astype(BF16)
    counts = lax.dot_general(
        named.astype(BF16), before, (((1,), (0,)), ((), ())), preferred_element_type=F32
    )
    return named.astype(BF16), jnp.sum(named * counts, axis=0, keepdims=True).astype(jnp.int32)


def pack_messages(columns, tiles, cells):
    row = iota((8, PROFS), 0)
    zero = jnp.zeros((8, PROFS), F32)
    named, ranks, tops, rests, yx = [], [], [], [], []
    for w in range(ITERS):
        n, rank = rank_in_tile(tiles[w])
        named += [n, n]
        ranks.append(rank)
        top = [c.astype(BF16).astype(F32) for c in columns[w]]
        tops.append(top)
        rests.append([c - t for c, t in zip(columns[w], top)])
        cell = cells[w]
        yx.append(jnp.where(row % 2 == 0, (cell // LANES).astype(F32), (cell % LANES).astype(F32)))
    high = [[], []]
    low = [[], []]

    def add(w, top, rest):
        for u in range(ITERS):
            high[u].append(top if u == w else zero)
            low[u].append(rest if u == w else zero)

    for upper in range(RANK_ROWS):
        for w in range(ITERS):
            for v in range(VARS):
                for r in range(RANKS):
                    here = ranks[w] == upper * RANKS + r
                    add(w, jnp.where(here, tops[w][v], 0.0), jnp.where(here, rests[w][v], 0.0))
    for upper in range(RANK_ROWS):
        for w in range(ITERS):
            add(w, jnp.where(ranks[w] == upper * RANKS + row // 2, yx[w], 0.0), zero)
        add(0, zero, zero)
        add(0, zero, zero)
    values = jnp.concatenate(
        [jnp.concatenate(part[w], axis=0).astype(BF16) for w in range(ITERS) for part in (high, low)], axis=1
    )
    return dot_nt(jnp.concatenate(named, axis=1), values)


def gather_cells(received):
    got = jnp.concatenate([received(j) for j in range(RANK_ROWS)], axis=0).T
    cells = received(RANK_ROWS)
    where_ = jnp.concatenate([roll_lanes(cells, -32 * j) for j in range(RANK_ROWS)], axis=0).T
    top = got.astype(BF16).astype(F32)
    rest = got - top
    y_of_row = iota((ROWS, LANES), 0).astype(F32)
    x_of_row = iota((LANES, LANES), 0).astype(F32)
    out = []
    for w in range(ITERS):
        left, right = [], []
        for r in range(RANKS):
            at = (w * RANKS + r) * 2
            y_here = where_[at : at + 1] == y_of_row
            x_here = (where_[at + 1 : at + 2] == x_of_row).astype(F32).astype(BF16)
            for part in (top, rest):
                blocks = []
                for v in range(VARS):
                    for l in range(LEV):
                        at = w * 64 + v * 32 + r * LEV + l
                        blocks.append(jnp.where(y_here, part[at : at + 1], 0.0))
                left.append(jnp.concatenate(blocks, axis=0).astype(BF16))
                right.append(x_here)
        out.append(dot_nt(jnp.concatenate(left, axis=1), jnp.concatenate(right, axis=1)))
    return out


def pack_edges(items):
    lane = iota((ROWS, LANES), 1)
    last = jnp.zeros((ROWS, LANES), F32)
    first = jnp.zeros((ROWS, LANES), F32)
    for slot, level, rows in items:
        at = 16 * level + 4 * slot
        turned = roll_lanes(rows, at + 4)
        last = jnp.where(jnp.logical_and(lane >= at, lane < at + 4), turned, last)
        first = jnp.where(jnp.logical_and(lane >= at + 4, lane < at + 8), turned, first)
    return last, first


def strip(slot, from_left, own_last, own_first, from_right):
    group = iota((ROWS, LANES), 1) % 16
    low = jnp.where(group < 4, roll_lanes(from_left, -4 * slot), roll_lanes(own_first, -4 * slot))
    high = jnp.where(group < 12, roll_lanes(own_last, 8 - 4 * slot), roll_lanes(from_right, 8 - 4 * slot))
    return jnp.where(group < 8, low, high)


def strips(slots, received, own):
    upper = iota((ROWS, LANES), 0) < 4
    left_halo = jnp.where(upper, received[1], received[2])
    right_halo = jnp.where(upper, received[4], received[5])
    sides = ((received[0], received[3]), (left_halo, right_halo))
    return [
        tuple(strip(slot, sides[t][0], own[t][0], own[t][1], sides[t][1]) for t in range(2)) for slot in slots
    ]


def y_neighbours(pair):
    row = iota((ROWS, LANES), 0)
    a, b = pair
    next_a, next_b = pltpu.roll(a, ROWS - 1, 0), pltpu.roll(b, ROWS - 1, 0)
    prev_a, prev_b = pltpu.roll(a, 1, 0), pltpu.roll(b, 1, 0)
    plus = (jnp.where(row == ROWS - 1, next_b, next_a), jnp.where(row == ROWS - 1, next_a, next_b))
    minus = (jnp.where(row == 0, prev_b, prev_a), jnp.where(row == 0, prev_a, prev_b))
    return plus, minus


def edge_pair(one):
    group = iota((ROWS, LANES), 1) % 16
    return jnp.where(group == 13, roll_lanes(one, 10), one)


def x_neighbours(one, edges, level):
    lane = iota((ROWS, LANES), 1)
    halo = roll_lanes(edges, LANES - 1 - 12 - 16 * level)
    plus = jnp.where(lane == LANES - 1, halo, roll_lanes(one, -1))
    minus = jnp.where(lane == 0, halo, roll_lanes(one, 1))
    return plus, minus


def strip_x_neighbours(one):
    return roll_lanes(one, -1), roll_lanes(one, 1)


def weights_of(diff, ocean, x_pairs):
    (diff_n, ocean_n) = (y_neighbours(diff), y_neighbours(ocean))
    out = []
    for t in range(2):
        near = [(diff_n[0][t], ocean_n[0][t]), (diff_n[1][t], ocean_n[1][t])] + list(x_pairs[t])
        faces = [0.5 * (diff[t] + d) * ocean[t] * o for d, o in near]
        out.append((1.0 - (faces[0] + faces[1] + faces[2] + faces[3]), faces))
    return out


def lateral(one, near, weights):
    centre, faces = weights
    total = centre * one
    for face, value in zip(faces, near):
        total = total + face * value
    return total


def couple(diffused, coef, ocean):
    out = []
    for f in range(F):
        total = None
        for g in range(F):
            if diffused[g] is not None:
                term = coef[g][f] * diffused[g]
                total = term if total is None else total + term
        out.append(ocean * total)
    return out


def step_strips(old, weights, vertical, ocean, coef):
    lane = iota((ROWS, LANES), 1)
    diffused = [[None] * F, [None] * F]
    for f in range(F):
        if old[f] is None:
            continue
        plus, minus = y_neighbours(old[f])
        for t in range(2):
            one = old[f][t]
            x_plus, x_minus = strip_x_neighbours(one)
            below = jnp.where(lane < LANES - 16, roll_lanes(one, -16), 0.0)
            flux = vertical[t] * (below - one)
            above = jnp.where(lane < 16, 0.0, roll_lanes(flux, 16))
            diffused[t][f] = lateral(one, (plus[t], minus[t], x_plus, x_minus), weights[t]) + (flux - above)
    coupled = [couple(diffused[t], coef, ocean[t]) for t in range(2)]
    return [(coupled[0][f], coupled[1][f]) for f in range(F)]


def step_tile(read, write, live, edges, weights, vertical, ocean, coef, tiles):
    above = [[None] * F, [None] * F]
    for l in range(LEV):
        diffused = [[None] * F, [None] * F]
        for f in range(F):
            here = read(f, l) if (f, l) in live else None
            below = read(f, l + 1) if (f, l + 1) in live else None
            near = y_neighbours(here) if here is not None else None
            for t in range(tiles):
                flux = None
                if here is not None and below is not None:
                    flux = vertical(l, t) * (below[t] - here[t])
                elif here is not None:
                    flux = -(vertical(l, t) * here[t])
                elif below is not None:
                    flux = vertical(l, t) * below[t]
                total = None
                if here is not None:
                    x_plus, x_minus = x_neighbours(here[t], edges[f][t], l)
                    total = lateral(here[t], (near[0][t], near[1][t], x_plus, x_minus), weights[t])
                if flux is not None:
                    total = flux if total is None else total + flux
                if above[t][f] is not None:
                    total = -above[t][f] if total is None else total - above[t][f]
                above[t][f] = flux
                diffused[t][f] = total
        for t in range(tiles):
            for f, value in enumerate(couple(diffused[t], coef, ocean[t])):
                write(f, l, t, value)


def kernel(
    sizes,
    innov,
    weight,
    level,
    tile,
    cell,
    land,
    hdiff,
    vdiff,
    coupling,
    ice,
    out,
    innov_v,
    weight_v,
    level_v,
    tile_v,
    cell_v,
    land_v,
    coupling_v,
    ice_v,
    stat,
    stat_y,
    stat_e,
    stat_x,
    send,
    recv,
    forced,
    forced_y,
    forced_e,
    forced_x,
    border,
    border_ice,
    border_land,
    border_e,
    state,
    local_sem,
    send_sem,
    recv_sem,
    later_sem,
):
    n_ty, n_tx, n_grp = sizes
    ty, tx, grp = lax.axis_index("ty"), lax.axis_index("tx"), lax.axis_index("grp")
    blocks = n_tx * n_grp
    block = tx * n_grp + grp
    right, left = (block + 1) % blocks, (block + blocks - 1) % blocks
    down, up = (ty + 1) % n_ty, (ty + n_ty - 1) % n_ty

    def at(row, column):
        return (row, column // n_grp, column % n_grp)

    half = n_tx // 2
    z = tx % half
    at_first = jnp.logical_and(z == 0, grp == 0)
    at_last = jnp.logical_and(z == half - 1, grp == 1)

    def z_of(column):
        return (column // n_grp) % half

    def fetch(src, dst, sem):
        copy = pltpu.make_async_copy(src, dst, local_sem.at[sem])
        copy.start()
        return copy

    def put(src, dst, sem, device):
        pltpu.make_async_remote_copy(
            src_ref=src,
            dst_ref=dst,
            send_sem=send_sem.at[sem],
            recv_sem=recv_sem.at[sem],
            device_id=device,
            device_id_type=MESH,
        ).start()

    def wait(ref, sems, sem):
        pltpu.make_async_copy(ref, ref, sems.at[sem]).wait()

    def signal(sem, device):
        pl.semaphore_signal(sem, inc=1, device_id=device, device_id_type=MESH)

    def peers(low, high, act):
        def one(i, carry):
            for side in range(2):
                peer = i + side * half

                @pl.when(peer != tx)
                def _():
                    act(peer)

            return carry

        lax.fori_loop(low, high, one, 0)

    if n_tx < SLOTS:
        recv[...] = jnp.zeros(recv.shape, F32)
        border[...] = jnp.zeros(border.shape, F32)

    loads = [
        fetch(level, level_v, L_LEVEL),
        fetch(weight, weight_v, L_WEIGHT),
        fetch(innov, innov_v, L_INNOV),
        fetch(tile, tile_v, L_TILE),
        fetch(cell, cell_v, L_CELL),
    ]
    ice_here = ice.at[:, :, :, pl.ds(pl.multiple_of(grp * LANES, LANES), LANES)]
    ice_there = ice.at[:, :, :, pl.ds(pl.multiple_of((1 - grp) * LANES, LANES), LANES)]
    ice_last = ice.at[:, :, :, pl.ds((n_grp - 1) * LANES, LANES)]
    static_loads = [
        fetch(land, land_v, L_LAND),
        fetch(hdiff, stat.at[LEV], L_HDIFF),
        fetch(vdiff, stat.at[pl.ds(0, LEV)], L_VDIFF),
        fetch(ice_here, ice_v.at[grp], L_ICE),
        fetch(coupling, coupling_v, L_COUPLING),
    ]

    barrier = pltpu.get_barrier_semaphore()
    z_right, z_left = z_of(right), z_of(left)
    peers(z, half, lambda peer: signal(barrier, (ty, peer, grp)))
    signal(barrier, at(down, block))
    signal(barrier, at(up, block))
    for column, z_there in ((right, z_right), (left, z_left)):

        @pl.when(z_there >= z)
        def _():
            for r in (ty, down, up):
                signal(barrier, at(r, column))

    @pl.when(at_first)
    def _():
        def source(k, carry):
            signal(barrier, (ty, k, 1))
            return carry

        lax.fori_loop(0, n_tx, source, 0)
        signal(barrier, (ty, (tx + n_tx - 1) % n_tx, 0))

    earlier = 1 + 2 * z + 2 + jnp.where(z_right <= z, 3, 0) + jnp.where(z_left <= z, 3, 0)
    earlier = earlier + jnp.where(grp == 1, 2, 0)
    earlier = earlier + jnp.where(jnp.logical_and(z == half - 1, grp == 0), 1, 0)
    later = 2 * (half - 1 - z) + jnp.where(z_right > z, 3, 0) + jnp.where(z_left > z, 3, 0)
    pl.semaphore_wait(barrier, earlier)
    peers(0, z, lambda peer: signal(later_sem, (ty, peer, grp)))
    for column, z_there in ((right, z_right), (left, z_left)):

        @pl.when(z_there < z)
        def _():
            for r in (ty, down, up):
                signal(later_sem, at(r, column))

    for load in loads:
        load.wait()
    columns = [
        level_sums(
            weight_v[w],
            level_v[w],
            [innov_v[pl.ds(w * PROFS * VARS + v, PROFS, stride=VARS), :] for v in range(VARS)],
        )
        for w in range(ITERS)
    ]
    messages = pack_messages(
        columns, [tile_v[pl.ds(w, 1), :] for w in range(ITERS)], [cell_v[pl.ds(w, 1), :] for w in range(ITERS)]
    )
    for j in range(MESSAGE):
        send[:, j, :] = messages[:, j * LANES : (j + 1) * LANES]

    def route(peer):
        put(send.at[peer], recv.at[tx], R_ROUTE, (ty, peer, grp))

    @pl.when(grp == 1)
    def _():
        for side in range(2):
            last = half - 1 + side * half
            put(send.at[last], border.at[tx], R_BORDER, (ty, (last + 1) % n_tx, 0))

    peers(0, z + 1, route)
    own = fetch(send.at[tx], recv.at[tx], L_OWN)
    for load in static_loads:
        load.wait()
    ocean_tile = land_v[...].astype(F32)
    stat[LEV + 1] = ocean_tile

    @pl.when(z == half - 1)
    def _():
        put(ice_last, border_ice.at[grp], R_BORDER_ICE, (ty, (tx + 1) % n_tx, 0))

    @pl.when(at_last)
    def _():
        put(stat.at[LEV + 1], border_land, R_BORDER_LAND, (ty, (tx + 1) % n_tx, 0))

    put(ice_there, ice_v.at[grp], R_ICE, (ty, tx, 1 - grp))

    def static_items(ref):
        items = [(0, l, ref[l]) for l in range(LEV)]
        return items + [(1 + j, l, ref[LEV + j]) for j in range(2) for l in range(LEV)]

    last, first = pack_edges(static_items(stat))
    stat_e[0] = last
    stat_e[1] = first


    @pl.when(later > 0)
    def _():
        pl.semaphore_wait(later_sem, later)

    peers(z + 1, half, route)

    def exchange_y(rows, rows_y, sem):
        put(rows.at[:, pl.ds(0, 4)], rows_y.at[:, pl.ds(0, 4)], sem, at(up, block))
        put(rows.at[:, pl.ds(4, 4)], rows_y.at[:, pl.ds(4, 4)], sem, at(down, block))

    exchange_y(stat, stat_y, R_STAT_Y)
    for side, column in enumerate((right, left)):
        for slot, r in enumerate((ty, up, down)):
            put(stat_e.at[side], stat_x.at[side * 3 + slot], R_STAT_X, at(r, column))

    def force(received, melt_of, ocean_of):
        sums = gather_cells(received)
        rows = []
        for w in range(ITERS):
            rows.append([])
            for i, (f, l) in enumerate(FORCED):
                value = sums[w][i * ROWS : (i + 1) * ROWS] if f < VARS else None
                if l == 0:
                    melt = jnp.concatenate([melt_of[0, w, f], melt_of[1, w, f]], axis=0)
                    value = melt if value is None else value + melt
                rows[w].append(ocean_of * value)
        return rows

    def edges_of(rows):
        return pack_edges([(f, l, rows[i]) for i, (f, l) in enumerate(FORCED)])

    own.wait()
    wait(recv.at[pl.ds(0, n_tx - 1)], recv_sem, R_ROUTE)
    wait(ice_v.at[0], recv_sem, R_ICE)
    rows = force(lambda j: recv[:, j, :], ice_v, ocean_tile)
    for w in range(ITERS):
        for i in range(N_FORCED):
            forced[w * N_FORCED + i] = rows[w][i]
    exchange_y(forced, forced_y, R_FORCED_Y)
    for w in range(ITERS):
        last, first = edges_of(rows[w])
        forced_e[0, w] = last
        forced_e[1, w] = first

    def exchange_x(side, column, sem):
        for slot, r in enumerate((ty, up, down)):
            put(forced_e.at[side], forced_x.at[side * 3 + slot], sem, at(r, column))

    exchange_x(1, left, R_FORCED_LEFT)

    @pl.when(jnp.logical_not(at_last))
    def _():
        exchange_x(0, right, R_FORCED_RIGHT)

    @pl.when(at_first)
    def _():
        wait(border.at[pl.ds(0, n_tx)], recv_sem, R_BORDER)
        wait(border_ice, recv_sem, R_BORDER_ICE)
        wait(border_land, recv_sem, R_BORDER_LAND)
        beyond = force(lambda j: border[:, j, :], border_ice, border_land[...])
        for w in range(ITERS):
            edge = edges_of(beyond[w])[0]
            border_e[w] = edge
            forced_x[0, w] = edge
        for slot, r in ((1, up), (2, down)):
            put(border_e, forced_x.at[slot], R_FORCED_RIGHT, at(r, block))

    wait(stat_y, recv_sem, R_STAT_Y)
    wait(stat_x, recv_sem, R_STAT_X)
    own_edges = ((stat_e[0], stat_e[1]), pack_edges(static_items(stat_y)))
    vertical_s, diff_s, ocean_s = strips((0, 1, 2), [stat_x[i] for i in range(6)], own_edges)
    diff = (stat[LEV], stat_y[LEV])
    ocean = (stat[LEV + 1], stat_y[LEV + 1])
    x_pairs, x_pairs_s = [], []
    for t in range(2):
        d = x_neighbours(diff[t], edge_pair(diff_s[t]), 0)
        o = x_neighbours(ocean[t], edge_pair(ocean_s[t]), 0)
        x_pairs.append(((d[0], o[0]), (d[1], o[1])))
        d, o = strip_x_neighbours(diff_s[t]), strip_x_neighbours(ocean_s[t])
        x_pairs_s.append(((d[0], o[0]), (d[1], o[1])))
    weights = weights_of(diff, ocean, x_pairs)
    weights_s = weights_of(diff_s, ocean_s, x_pairs_s)
    coef = [
        [
            jnp.broadcast_to(coupling_v[g : g + 1, f : f + 1], (ROWS, LANES)) + (1.0 if f == g else 0.0)
            for f in range(F)
        ]
        for g in range(F)
    ]

    def vertical(l, t):
        return stat[l] if t == 0 else stat_y[l]

    wait(forced_y, recv_sem, R_FORCED_Y)
    wait(forced_x.at[pl.ds(3, 3)], recv_sem, R_FORCED_LEFT)

    @pl.when(at_first)
    def _():
        wait(forced_x.at[pl.ds(1, 2)], recv_sem, R_FORCED_RIGHT)

    @pl.when(jnp.logical_not(at_first))
    def _():
        wait(forced_x.at[pl.ds(0, 3)], recv_sem, R_FORCED_RIGHT)

    def forced_strips(w):
        halo = edges_of([forced_y[w * N_FORCED + i] for i in range(N_FORCED)])
        own_edges = ((forced_e[0, w], forced_e[1, w]), halo)
        return strips(range(ICEV), [forced_x[i, w] for i in range(6)], own_edges)

    index = {item: i for i, item in enumerate(FORCED)}
    whole = {(f, l) for f in range(F) for l in range(LEV)}
    packed = forced_strips(0) + [None]

    def read_forced(f, l):
        return forced[index[f, l]], forced_y[index[f, l]]

    def reader(slot):
        return lambda f, l: (state[slot, 0, f * LEV + l], state[slot, 1, f * LEV + l])

    def writer(slot):
        def write(f, l, t, value):
            state[slot, t, f * LEV + l] = value

        return write

    def write_out(f, l, t, value):
        out[f, l] = value

    n_steps = ITERS * SUB
    for step in range(n_steps):
        end = step == n_steps - 1
        edges = [None if p is None else (edge_pair(p[0]), edge_pair(p[1])) for p in packed]
        step_tile(
            read_forced if step == 0 else reader(step % 2),
            write_out if end else writer((step + 1) % 2),
            set(FORCED) if step == 0 else whole,
            edges,
            weights,
            vertical,
            ocean,
            coef,
            1 if end else 2,
        )
        if not end:
            packed = step_strips(packed, weights_s, vertical_s, ocean_s, coef)
        if step == SUB - 1:
            slot = (step + 1) % 2
            added = forced_strips(1)
            for f in range(ICEV):
                packed[f] = tuple(packed[f][t] + added[f][t] for t in range(2))
            for i, (f, l) in enumerate(FORCED):
                state[slot, 0, f * LEV + l] += forced[N_FORCED + i]
                state[slot, 1, f * LEV + l] += forced_y[N_FORCED + i]

    wait(send.at[pl.ds(0, n_tx - 1)], send_sem, R_ROUTE)
    wait(ice_v.at[0], send_sem, R_ICE)
    wait(stat, send_sem, R_STAT_Y)
    wait(stat_x, send_sem, R_STAT_X)
    wait(forced, send_sem, R_FORCED_Y)
    wait(forced_x.at[pl.ds(0, 3)], send_sem, R_FORCED_LEFT)

    @pl.when(jnp.logical_not(at_last))
    def _():
        wait(forced_x.at[pl.ds(0, 3)], send_sem, R_FORCED_RIGHT)

    @pl.when(at_first)
    def _():
        wait(forced_x.at[pl.ds(0, 2)], send_sem, R_FORCED_RIGHT)

    @pl.when(grp == 1)
    def _():
        wait(send.at[pl.ds(0, 2)], send_sem, R_BORDER)

    @pl.when(z == half - 1)
    def _():
        wait(border_ice.at[0], send_sem, R_BORDER_ICE)

    @pl.when(at_last)
    def _():
        wait(border_land, send_sem, R_BORDER_LAND)


def per_device(sizes, innov, weight, level, tile, cell, land, hdiff, vdiff, coupling, ice):
    scratch = [
        pltpu.VMEM((ITERS * PROFS * VARS, DEPTH), F32),
        pltpu.VMEM((ITERS, PROFS, DEPTH), F32),
        pltpu.VMEM((ITERS, PROFS, DEPTH), jnp.int32),
        pltpu.VMEM((ITERS, PROFS), jnp.int32),
        pltpu.VMEM((ITERS, PROFS), jnp.int32),
        pltpu.VMEM((ROWS, LANES), jnp.int32),
        pltpu.VMEM((F, F), F32),
        pltpu.VMEM((2, ITERS, ICEV, 4, LANES), F32),
        pltpu.VMEM((N_STATIC, ROWS, LANES), F32),
        pltpu.VMEM((N_STATIC, ROWS, LANES), F32),
        pltpu.VMEM((2, ROWS, LANES), F32),
        pltpu.VMEM((6, ROWS, LANES), F32),
        pltpu.VMEM((SLOTS, MESSAGE, LANES), F32),
        pltpu.VMEM((SLOTS, MESSAGE, LANES), F32),
        pltpu.VMEM((ITERS * N_FORCED, ROWS, LANES), F32),
        pltpu.VMEM((ITERS * N_FORCED, ROWS, LANES), F32),
        pltpu.VMEM((2, ITERS, ROWS, LANES), F32),
        pltpu.VMEM((6, ITERS, ROWS, LANES), F32),
        pltpu.VMEM((SLOTS, MESSAGE, LANES), F32),
        pltpu.VMEM((2, ITERS, ICEV, 4, LANES), F32),
        pltpu.VMEM((ROWS, LANES), F32),
        pltpu.VMEM((ITERS, ROWS, LANES), F32),
        pltpu.VMEM((2, 2, F * LEV, ROWS, LANES), F32),
        pltpu.SemaphoreType.DMA((N_LOCAL,)),
        pltpu.SemaphoreType.DMA((N_REMOTE,)),
        pltpu.SemaphoreType.DMA((N_REMOTE,)),
        pltpu.SemaphoreType.REGULAR,
    ]
    operands = (
        innov.reshape(ITERS * PROFS * VARS, DEPTH),
        weight,
        level,
        tile.reshape(ITERS, PROFS),
        cell,
        land,
        hdiff,
        vdiff,
        coupling,
        ice,
    )
    anywhere = pl.BlockSpec(memory_space=pltpu.HBM)
    return pl.pallas_call(
        functools.partial(kernel, sizes),
        out_shape=jax.ShapeDtypeStruct((F, LEV, ROWS, LANES), F32),
        in_specs=[anywhere] * len(operands),
        out_specs=pl.BlockSpec(memory_space=pltpu.VMEM),
        scratch_shapes=scratch,
        compiler_params=pltpu.CompilerParams(
            collective_id=0, has_side_effects=True, vmem_limit_bytes=16 * 1024 * 1024
        ),
    )(*(pltpu.with_memory_space_constraint(operand, pltpu.HBM) for operand in operands))


def solution(mesh):
    sizes = tuple(mesh.shape[axis] for axis in ("ty", "tx", "grp"))
    in_specs = (
        P(None, ("ty", "tx", "grp"), None, None),
        P(None, ("ty", "tx", "grp"), None),
        P(None, ("ty", "tx", "grp"), None),
        P(None, ("ty", "tx", "grp"), None),
        P(None, ("ty", "tx", "grp")),
        P("ty", ("tx", "grp")),
        P("ty", ("tx", "grp")),
        P(None, "ty", ("tx", "grp")),
        P(),
        P(None, None, ("ty", "grp"), "tx"),
    )
    out_specs = P(None, None, "ty", ("tx", "grp"))
    return jax.shard_map(
        functools.partial(per_device, sizes), mesh=mesh, in_specs=in_specs, out_specs=out_specs, check_vma=False
    )
```

```python
import functools

import jax
import jax.numpy as jnp
from jax import lax
from jax.experimental import pallas as pl
from jax.experimental.pallas import tpu as pltpu
from jax.sharding import PartitionSpec as P

F = 5
LEV = 8
VARS = 2
ICEV = 4
ROWS = 8
LANES = 128
DEPTH = 128
PROFS = 128
ITERS = 2
SUB = 2
SLOTS = 32
N_FORCED = VARS * LEV + (ICEV - VARS)
N_STATIC = LEV + 2
MESH = pl.DeviceIdType.MESH
F32 = jnp.float32
BF16 = jnp.bfloat16
NT = (((1,), (1,)), ((), ()))

FORCED = [(f, l) for f in range(VARS) for l in range(LEV)] + [(f, 0) for f in range(VARS, ICEV)]

L_LEVEL, L_WEIGHT, L_INNOV, L_TILE, L_CELL, L_LAND, L_HDIFF, L_VDIFF, L_ICE, L_COUPLING, L_OWN = range(11)
N_LOCAL = 11
R_ROUTE, R_ICE, R_STAT_Y, R_STAT_X, R_FORCED_Y, R_FORCED_RIGHT, R_FORCED_LEFT = range(7)
R_BORDER, R_BORDER_ICE, R_BORDER_LAND, R_STAT_YE, R_FORCED_YE = range(7, 12)
N_REMOTE = 12
GROUPS = 3
S_NEAR, S_DIAGONAL = GROUPS, GROUPS + 1

RANK_ROWS = 4
RANKS = 4
MESSAGE = RANK_ROWS + 1


def iota(shape, axis):
    return lax.broadcasted_iota(jnp.int32, shape, axis)


def split(x):
    high = x.astype(BF16)
    low = (x - high.astype(F32)).astype(BF16)
    return high, low


def roll_lanes(x, shift):
    shift %= LANES
    return x if shift == 0 else pltpu.roll(x, shift, 1)


def dot_nt(a, b):
    return lax.dot_general(a, b, NT, preferred_element_type=F32)


def level_sums(weight, level, innovs):
    level_t = level.T
    out = []
    for innov in innovs:
        weighted_t = (weight * innov).T
        rows = [
            jnp.sum(jnp.where(level_t == l, weighted_t, 0.0), axis=0, keepdims=True) for l in range(LEV)
        ]
        out.append(jnp.concatenate(rows, axis=0))
    return out


def rank_in_tile(tile):
    named = (tile == iota((SLOTS, PROFS), 0)).astype(F32)
    before = (iota((PROFS, PROFS), 0) < iota((PROFS, PROFS), 1)).astype(F32).astype(BF16)
    counts = lax.dot_general(
        named.astype(BF16), before, (((1,), (0,)), ((), ())), preferred_element_type=F32
    )
    return named.astype(BF16), jnp.sum(named * counts, axis=0, keepdims=True).astype(jnp.int32)


def pack_messages(columns, tiles, cells):
    row = iota((8, PROFS), 0)
    zero = jnp.zeros((8, PROFS), F32)
    named, ranks, tops, rests, yx = [], [], [], [], []
    for w in range(ITERS):
        n, rank = rank_in_tile(tiles[w])
        named += [n, n]
        ranks.append(rank)
        top = [c.astype(BF16).astype(F32) for c in columns[w]]
        tops.append(top)
        rests.append([c - t for c, t in zip(columns[w], top)])
        cell = cells[w]
        yx.append(jnp.where(row % 2 == 0, (cell // LANES).astype(F32), (cell % LANES).astype(F32)))
    high = [[], []]
    low = [[], []]

    def add(w, top, rest):
        for u in range(ITERS):
            high[u].append(top if u == w else zero)
            low[u].append(rest if u == w else zero)

    for upper in range(RANK_ROWS):
        for w in range(ITERS):
            for v in range(VARS):
                for r in range(RANKS):
                    here = ranks[w] == upper * RANKS + r
                    add(w, jnp.where(here, tops[w][v], 0.0), jnp.where(here, rests[w][v], 0.0))
    for upper in range(RANK_ROWS):
        for w in range(ITERS):
            add(w, jnp.where(ranks[w] == upper * RANKS + row // 2, yx[w], 0.0), zero)
        add(0, zero, zero)
        add(0, zero, zero)
    values = jnp.concatenate(
        [jnp.concatenate(part[w], axis=0).astype(BF16) for w in range(ITERS) for part in (high, low)], axis=1
    )
    return dot_nt(jnp.concatenate(named, axis=1), values)


def gather_cells(received):
    got = jnp.concatenate([received(j) for j in range(RANK_ROWS)], axis=0).T
    cells = received(RANK_ROWS)
    where_ = jnp.concatenate([roll_lanes(cells, -32 * j) for j in range(RANK_ROWS)], axis=0).T
    top = got.astype(BF16).astype(F32)
    rest = got - top
    y_of_row = iota((ROWS, LANES), 0).astype(F32)
    x_of_row = iota((LANES, LANES), 0).astype(F32)
    out = []
    for w in range(ITERS):
        left, right = [], []
        for r in range(RANKS):
            at = (w * RANKS + r) * 2
            y_here = where_[at : at + 1] == y_of_row
            x_here = (where_[at + 1 : at + 2] == x_of_row).astype(F32).astype(BF16)
            for part in (top, rest):
                blocks = []
                for v in range(VARS):
                    for l in range(LEV):
                        at = w * 64 + v * 32 + r * LEV + l
                        blocks.append(jnp.where(y_here, part[at : at + 1], 0.0))
                left.append(jnp.concatenate(blocks, axis=0).astype(BF16))
                right.append(x_here)
        out.append(dot_nt(jnp.concatenate(left, axis=1), jnp.concatenate(right, axis=1)))
    return out


def gather_edges(received):
    got = jnp.concatenate([received(j) for j in range(RANK_ROWS)], axis=0).T
    cells = received(RANK_ROWS)
    where_ = jnp.concatenate([roll_lanes(cells, -32 * j) for j in range(RANK_ROWS)], axis=0).T
    top = got.astype(BF16).astype(F32)
    rest = got - top
    row = iota((ROWS, LANES), 0)
    y_of_row = row.astype(F32)
    x_of_row = (LANES - 4 + row % 4).astype(F32)
    zero = jnp.zeros((ROWS, LANES), F32)
    out = []
    for w in range(ITERS):
        left, right = [], []
        for r in range(RANKS):
            at = (w * RANKS + r) * 2
            y_here = (where_[at : at + 1] == y_of_row).astype(F32)
            x_here = where_[at + 1 : at + 2] == x_of_row
            for part in (top, rest):
                blocks = []
                for l in range(LEV):
                    at = w * 64 + r * LEV + l
                    both = jnp.where(row < 4, part[at : at + 1], part[at + 32 : at + 33])
                    blocks += [jnp.where(x_here, both, 0.0), zero]
                left.append(y_here)
                right.append(jnp.concatenate(blocks, axis=0).astype(BF16))
        out.append(
            dot_nt(jnp.concatenate(left, axis=1).astype(BF16), jnp.concatenate(right, axis=1))
        )
    return out


def pack_edges(items):
    lane = iota((ROWS, LANES), 1)
    last = jnp.zeros((ROWS, LANES), F32)
    first = jnp.zeros((ROWS, LANES), F32)
    for slot, level, rows in items:
        at = 16 * level + 4 * slot
        turned = roll_lanes(rows, at + 4)
        last = jnp.where(jnp.logical_and(lane >= at, lane < at + 4), turned, last)
        first = jnp.where(jnp.logical_and(lane >= at + 4, lane < at + 8), turned, first)
    return last, first


def strip(slot, from_left, own_last, own_first, from_right):
    group = iota((ROWS, LANES), 1) % 16
    low = jnp.where(group < 4, roll_lanes(from_left, -4 * slot), roll_lanes(own_first, -4 * slot))
    high = jnp.where(group < 12, roll_lanes(own_last, 8 - 4 * slot), roll_lanes(from_right, 8 - 4 * slot))
    return jnp.where(group < 8, low, high)


def strips(slots, received, own):
    upper = iota((ROWS, LANES), 0) < 4
    left_halo = jnp.where(upper, received[1], received[2])
    right_halo = jnp.where(upper, received[4], received[5])
    sides = ((received[0], received[3]), (left_halo, right_halo))
    return [
        tuple(strip(slot, sides[t][0], own[t][0], own[t][1], sides[t][1]) for t in range(2)) for slot in slots
    ]


def y_neighbours(pair):
    row = iota((ROWS, LANES), 0)
    a, b = pair
    next_a, next_b = pltpu.roll(a, ROWS - 1, 0), pltpu.roll(b, ROWS - 1, 0)
    prev_a, prev_b = pltpu.roll(a, 1, 0), pltpu.roll(b, 1, 0)
    plus = (jnp.where(row == ROWS - 1, next_b, next_a), jnp.where(row == ROWS - 1, next_a, next_b))
    minus = (jnp.where(row == 0, prev_b, prev_a), jnp.where(row == 0, prev_a, prev_b))
    return plus, minus


def edge_pair(one):
    group = iota((ROWS, LANES), 1) % 16
    return jnp.where(group == 13, roll_lanes(one, 10), one)


def x_neighbours(one, edges, level):
    lane = iota((ROWS, LANES), 1)
    halo = roll_lanes(edges, LANES - 1 - 12 - 16 * level)
    plus = jnp.where(lane == LANES - 1, halo, roll_lanes(one, -1))
    minus = jnp.where(lane == 0, halo, roll_lanes(one, 1))
    return plus, minus


def strip_x_neighbours(one):
    return roll_lanes(one, -1), roll_lanes(one, 1)


def weights_of(diff, ocean, x_pairs):
    (diff_n, ocean_n) = (y_neighbours(diff), y_neighbours(ocean))
    out = []
    for t in range(2):
        near = [(diff_n[0][t], ocean_n[0][t]), (diff_n[1][t], ocean_n[1][t])] + list(x_pairs[t])
        faces = [0.5 * (diff[t] + d) * ocean[t] * o for d, o in near]
        out.append((1.0 - (faces[0] + faces[1] + faces[2] + faces[3]), faces))
    return out


def lateral(one, near, weights):
    centre, faces = weights
    total = centre * one
    for face, value in zip(faces, near):
        total = total + face * value
    return total


def couple(diffused, coef, ocean):
    out = []
    for f in range(F):
        total = None
        for g in range(F):
            if diffused[g] is not None:
                term = coef[g][f] * diffused[g]
                total = term if total is None else total + term
        out.append(ocean * total)
    return out


def step_strips(old, weights, vertical, ocean, coef):
    lane = iota((ROWS, LANES), 1)
    diffused = [[None] * F, [None] * F]
    for f in range(F):
        if old[f] is None:
            continue
        plus, minus = y_neighbours(old[f])
        for t in range(2):
            one = old[f][t]
            x_plus, x_minus = strip_x_neighbours(one)
            below = jnp.where(lane < LANES - 16, roll_lanes(one, -16), 0.0)
            flux = vertical[t] * (below - one)
            above = jnp.where(lane < 16, 0.0, roll_lanes(flux, 16))
            diffused[t][f] = lateral(one, (plus[t], minus[t], x_plus, x_minus), weights[t]) + (flux - above)
    coupled = [couple(diffused[t], coef, ocean[t]) for t in range(2)]
    return [(coupled[0][f], coupled[1][f]) for f in range(F)]


def step_tile(read, write, live, edges, weights, vertical, ocean, coef, tiles):
    above = [[None] * F, [None] * F]
    for l in range(LEV):
        diffused = [[None] * F, [None] * F]
        for f in range(F):
            here = read(f, l) if (f, l) in live else None
            below = read(f, l + 1) if (f, l + 1) in live else None
            near = y_neighbours(here) if here is not None else None
            for t in range(tiles):
                flux = None
                if here is not None and below is not None:
                    flux = vertical(l, t) * (below[t] - here[t])
                elif here is not None:
                    flux = -(vertical(l, t) * here[t])
                elif below is not None:
                    flux = vertical(l, t) * below[t]
                total = None
                if here is not None:
                    x_plus, x_minus = x_neighbours(here[t], edges[f][t], l)
                    total = lateral(here[t], (near[0][t], near[1][t], x_plus, x_minus), weights[t])
                if flux is not None:
                    total = flux if total is None else total + flux
                if above[t][f] is not None:
                    total = -above[t][f] if total is None else total - above[t][f]
                above[t][f] = flux
                diffused[t][f] = total
        for t in range(tiles):
            for f, value in enumerate(couple(diffused[t], coef, ocean[t])):
                write(f, l, t, value)


def kernel(
    sizes,
    innov,
    weight,
    level,
    tile,
    cell,
    land,
    hdiff,
    vdiff,
    coupling,
    ice,
    out,
    innov_v,
    weight_v,
    level_v,
    tile_v,
    cell_v,
    land_v,
    coupling_v,
    ice_v,
    stat,
    stat_y,
    stat_e,
    stat_x,
    send,
    recv,
    forced,
    forced_y,
    forced_e,
    forced_x,
    stat_ye,
    forced_ye,
    border,
    border_ice,
    border_land,
    border_e,
    state,
    local_sem,
    send_sem,
    recv_sem,
    enter_sem,
):
    n_ty, n_tx, n_grp = sizes
    ty, tx, grp = lax.axis_index("ty"), lax.axis_index("tx"), lax.axis_index("grp")
    blocks = n_tx * n_grp
    block = tx * n_grp + grp
    right, left = (block + 1) % blocks, (block + blocks - 1) % blocks
    down, up = (ty + 1) % n_ty, (ty + n_ty - 1) % n_ty

    def at(row, column):
        return (row, column // n_grp, column % n_grp)

    half = n_tx // 2
    z, side = tx % half, tx // half
    at_first = jnp.logical_and(z == 0, grp == 0)
    at_last = jnp.logical_and(z == half - 1, grp == 1)

    def z_of(column):
        return (column // n_grp) % half

    def fetch(src, dst, sem):
        copy = pltpu.make_async_copy(src, dst, local_sem.at[sem])
        copy.start()
        return copy

    def put(src, dst, sem, device):
        pltpu.make_async_remote_copy(
            src_ref=src,
            dst_ref=dst,
            send_sem=send_sem.at[sem],
            recv_sem=recv_sem.at[sem],
            device_id=device,
            device_id_type=MESH,
        ).start()

    def wait(ref, sems, sem):
        pltpu.make_async_copy(ref, ref, sems.at[sem]).wait()

    def signal(sem, device):
        pl.semaphore_signal(sem, inc=1, device_id=device, device_id_type=MESH)

    def peers(low, high, act):
        def one(i, carry):
            for half_of in range(2):
                act(i + half_of * half)
            return carry

        lax.fori_loop(low, high, one, 0)

    def turn_y(row):
        chip, chips = row // 2, n_ty // 2
        return 2 * jnp.where(chip < chips // 2, chip, chips + chips // 2 - 1 - chip) + 1 - row % 2

    def turn_x(column):
        return z_of(column) * 2 + column % n_grp

    nearest = [
        (at(down, block), turn_y(down) > turn_y(ty)),
        (at(up, block), turn_y(up) > turn_y(ty)),
        (at(ty, right), turn_x(right) > turn_x(block)),
        (at(ty, left), turn_x(left) > turn_x(block)),
    ]
    bounds = [0, half // 4, half // 2, half]
    group = jnp.where(z >= bounds[1], 1, 0) + jnp.where(z >= bounds[2], 1, 0)

    if n_tx < SLOTS:
        recv[...] = jnp.zeros(recv.shape, F32)
        border[...] = jnp.zeros(border.shape, F32)

    loads = [
        fetch(level, level_v, L_LEVEL),
        fetch(weight, weight_v, L_WEIGHT),
        fetch(innov, innov_v, L_INNOV),
        fetch(tile, tile_v, L_TILE),
        fetch(cell, cell_v, L_CELL),
    ]
    ice_here = ice.at[:, :, :, pl.ds(pl.multiple_of(grp * LANES, LANES), LANES)]
    ice_there = ice.at[:, :, :, pl.ds(pl.multiple_of((1 - grp) * LANES, LANES), LANES)]
    ice_last = ice.at[:, :, :, pl.ds((n_grp - 1) * LANES, LANES)]
    static_loads = [
        fetch(land, land_v, L_LAND),
        fetch(hdiff, stat.at[LEV], L_HDIFF),
        fetch(vdiff, stat.at[pl.ds(0, LEV)], L_VDIFF),
        fetch(ice_here, ice_v.at[grp], L_ICE),
        fetch(coupling, coupling_v, L_COUPLING),
    ]

    barrier = pltpu.get_barrier_semaphore()
    peers(z + 1, half, lambda peer: signal(barrier, (ty, peer, grp)))

    @pl.when(side == 0)
    def _():
        signal(barrier, (ty, tx + half, grp))

    for device, after in nearest:
        pl.when(after)(functools.partial(signal, barrier, device))

    @pl.when(at_first)
    def _():
        def source(k, carry):
            signal(barrier, (ty, k, 1))
            return carry

        lax.fori_loop(0, n_tx, source, 0)
        signal(barrier, (ty, (tx + n_tx - 1) % n_tx, 0))

    earlier = 2 * z + side + jnp.where(grp == 1, 2, 0)
    earlier = earlier + jnp.where(jnp.logical_and(z == half - 1, grp == 0), 1, 0)
    later_near = 0
    for _, after in nearest:
        earlier = earlier + jnp.where(after, 0, 1)
        later_near = later_near + jnp.where(after, 1, 0)

    def await_signals(sem, count):
        @pl.when(count > 0)
        def _():
            pl.semaphore_wait(sem, count)

    await_signals(barrier, earlier)
    peers(0, z, lambda peer: signal(enter_sem.at[group], (ty, peer, grp)))

    @pl.when(side == 1)
    def _():
        signal(enter_sem.at[group], (ty, tx - half, grp))

    for device, after in nearest:
        pl.when(jnp.logical_not(after))(functools.partial(signal, enter_sem.at[S_NEAR], device))

    for load in loads:
        load.wait()
    columns = [
        level_sums(
            weight_v[w],
            level_v[w],
            [innov_v[pl.ds(w * PROFS * VARS + v, PROFS, stride=VARS), :] for v in range(VARS)],
        )
        for w in range(ITERS)
    ]
    messages = pack_messages(
        columns, [tile_v[pl.ds(w, 1), :] for w in range(ITERS)], [cell_v[pl.ds(w, 1), :] for w in range(ITERS)]
    )
    for j in range(MESSAGE):
        send[:, j, :] = messages[:, j * LANES : (j + 1) * LANES]

    def route(peer):
        put(send.at[peer], recv.at[tx], R_ROUTE, (ty, peer, grp))

    @pl.when(grp == 1)
    def _():
        for side in range(2):
            last = half - 1 + side * half
            put(send.at[last], border.at[tx], R_BORDER, (ty, (last + 1) % n_tx, 0))

    peers(0, z, route)

    @pl.when(side == 1)
    def _():
        route(tx - half)

    own = fetch(send.at[tx], recv.at[tx], L_OWN)
    for load in static_loads:
        load.wait()
    ocean_tile = land_v[...].astype(F32)
    stat[LEV + 1] = ocean_tile

    @pl.when(z == half - 1)
    def _():
        put(ice_last, border_ice.at[grp], R_BORDER_ICE, (ty, (tx + 1) % n_tx, 0))

    @pl.when(at_last)
    def _():
        put(stat.at[LEV + 1], border_land, R_BORDER_LAND, (ty, (tx + 1) % n_tx, 0))

    def static_items(ref):
        items = [(0, l, ref[l]) for l in range(LEV)]
        return items + [(1 + j, l, ref[LEV + j]) for j in range(2) for l in range(LEV)]

    last, first = pack_edges(static_items(stat))
    stat_e[0] = last
    stat_e[1] = first

    def route_later(g):
        low, high = bounds[g], bounds[g + 1]
        start = jnp.maximum(z + 1, low)
        twin = jnp.logical_and(side == 0, group == g)
        await_signals(enter_sem.at[g], 2 * jnp.maximum(high - start, 0) + jnp.where(twin, 1, 0))
        peers(start, high, route)

        @pl.when(twin)
        def _():
            route(tx + half)

    for g in range(GROUPS - 1):
        route_later(g)
    await_signals(enter_sem.at[S_NEAR], later_near)
    for r in (up, down):
        signal(enter_sem.at[S_DIAGONAL], at(r, block))
    put(ice_there, ice_v.at[grp], R_ICE, (ty, tx, 1 - grp))
    route_later(GROUPS - 1)
    pl.semaphore_wait(enter_sem.at[S_DIAGONAL], 2)

    def exchange_y(rows, rows_y, sem):
        for r, part in ((up, pl.ds(0, 4)), (down, pl.ds(4, 4))):
            whole_ = (slice(None),) * (len(rows.shape) - 2)
            put(rows.at[*whole_, part], rows_y.at[*whole_, part], sem, at(r, block))

    exchange_y(stat, stat_y, R_STAT_Y)
    exchange_y(stat_e, stat_ye, R_STAT_YE)
    for edge, column in enumerate((right, left)):
        for slot, r in enumerate((ty, up, down)):
            put(stat_e.at[edge], stat_x.at[edge * 3 + slot], R_STAT_X, at(r, column))

    own.wait()
    wait(recv.at[pl.ds(0, n_tx - 1)], recv_sem, R_ROUTE)
    wait(ice_v.at[0], recv_sem, R_ICE)
    sums = gather_cells(lambda j: recv[:, j, :])
    rows = []
    for w in range(ITERS):
        rows.append([])
        for i, (f, l) in enumerate(FORCED):
            value = sums[w][i * ROWS : (i + 1) * ROWS] if f < VARS else None
            if l == 0:
                melt = jnp.concatenate([ice_v[0, w, f], ice_v[1, w, f]], axis=0)
                value = melt if value is None else value + melt
            rows[w].append(ocean_tile * value)
            forced[w * N_FORCED + i] = rows[w][i]
    exchange_y(forced, forced_y, R_FORCED_Y)
    for w in range(ITERS):
        last, first = pack_edges([(f, l, rows[w][i]) for i, (f, l) in enumerate(FORCED)])
        forced_e[0, w] = last
        forced_e[1, w] = first

    def exchange_x(edge, column, sem):
        for slot, r in enumerate((ty, up, down)):
            put(forced_e.at[edge], forced_x.at[edge * 3 + slot], sem, at(r, column))

    exchange_x(1, left, R_FORCED_LEFT)

    @pl.when(jnp.logical_not(at_last))
    def _():
        exchange_x(0, right, R_FORCED_RIGHT)

    exchange_y(forced_e, forced_ye, R_FORCED_YE)

    @pl.when(at_first)
    def _():
        wait(border_land, recv_sem, R_BORDER_LAND)
        wait(border_ice, recv_sem, R_BORDER_ICE)
        lane = iota((ROWS, LANES), 1)
        ocean_edge = jnp.where(lane < 4, roll_lanes(border_land[...], 4), 0.0)
        for width in (4, 8, 16, 32, 64):
            ocean_edge = ocean_edge + roll_lanes(ocean_edge, width)
        melts = []
        for w in range(ITERS):
            melt = jnp.zeros((ROWS, LANES), F32)
            for f in range(ICEV):
                tile_of = jnp.concatenate([border_ice[0, w, f], border_ice[1, w, f]], axis=0)
                here = jnp.logical_and(lane >= 4 * f, lane < 4 * f + 4)
                melt = jnp.where(here, roll_lanes(tile_of, 4 * f + 4), melt)
            melts.append(melt)
        wait(border.at[pl.ds(0, n_tx)], recv_sem, R_BORDER)
        sums = gather_edges(lambda j: border[:, j, :])
        for w in range(ITERS):
            edge = ocean_edge * (sums[w] + melts[w])
            border_e[w] = edge
            forced_x[0, w] = edge
        for slot, r in ((1, up), (2, down)):
            put(border_e, forced_x.at[slot], R_FORCED_RIGHT, at(r, block))

    wait(stat_y, recv_sem, R_STAT_Y)
    wait(stat_ye, recv_sem, R_STAT_YE)
    wait(stat_x, recv_sem, R_STAT_X)
    own_edges = ((stat_e[0], stat_e[1]), (stat_ye[0], stat_ye[1]))
    vertical_s, diff_s, ocean_s = strips((0, 1, 2), [stat_x[i] for i in range(6)], own_edges)
    diff = (stat[LEV], stat_y[LEV])
    ocean = (stat[LEV + 1], stat_y[LEV + 1])
    x_pairs, x_pairs_s = [], []
    for t in range(2):
        d = x_neighbours(diff[t], edge_pair(diff_s[t]), 0)
        o = x_neighbours(ocean[t], edge_pair(ocean_s[t]), 0)
        x_pairs.append(((d[0], o[0]), (d[1], o[1])))
        d, o = strip_x_neighbours(diff_s[t]), strip_x_neighbours(ocean_s[t])
        x_pairs_s.append(((d[0], o[0]), (d[1], o[1])))
    weights = weights_of(diff, ocean, x_pairs)
    weights_s = weights_of(diff_s, ocean_s, x_pairs_s)
    coef = [
        [
            jnp.broadcast_to(coupling_v[g : g + 1, f : f + 1], (ROWS, LANES)) + (1.0 if f == g else 0.0)
            for f in range(F)
        ]
        for g in range(F)
    ]

    def vertical(l, t):
        return stat[l] if t == 0 else stat_y[l]

    wait(forced_y, recv_sem, R_FORCED_Y)
    wait(forced_ye, recv_sem, R_FORCED_YE)
    wait(forced_x.at[pl.ds(3, 3)], recv_sem, R_FORCED_LEFT)

    @pl.when(at_first)
    def _():
        wait(forced_x.at[pl.ds(1, 2)], recv_sem, R_FORCED_RIGHT)

    @pl.when(jnp.logical_not(at_first))
    def _():
        wait(forced_x.at[pl.ds(0, 3)], recv_sem, R_FORCED_RIGHT)

    def forced_strips(w):
        own_edges = ((forced_e[0, w], forced_e[1, w]), (forced_ye[0, w], forced_ye[1, w]))
        return strips(range(ICEV), [forced_x[i, w] for i in range(6)], own_edges)

    index = {item: i for i, item in enumerate(FORCED)}
    whole = {(f, l) for f in range(F) for l in range(LEV)}
    packed = forced_strips(0) + [None]

    def read_forced(f, l):
        return forced[index[f, l]], forced_y[index[f, l]]

    def reader(slot):
        return lambda f, l: (state[slot, 0, f * LEV + l], state[slot, 1, f * LEV + l])

    def writer(slot):
        def write(f, l, t, value):
            state[slot, t, f * LEV + l] = value

        return write

    def write_out(f, l, t, value):
        out[f, l] = value

    n_steps = ITERS * SUB
    for step in range(n_steps):
        end = step == n_steps - 1
        edges = [None if p is None else (edge_pair(p[0]), edge_pair(p[1])) for p in packed]
        step_tile(
            read_forced if step == 0 else reader(step % 2),
            write_out if end else writer((step + 1) % 2),
            set(FORCED) if step == 0 else whole,
            edges,
            weights,
            vertical,
            ocean,
            coef,
            1 if end else 2,
        )
        if not end:
            packed = step_strips(packed, weights_s, vertical_s, ocean_s, coef)
        if step == SUB - 1:
            slot = (step + 1) % 2
            added = forced_strips(1)
            for f in range(ICEV):
                packed[f] = tuple(packed[f][t] + added[f][t] for t in range(2))
            for i, (f, l) in enumerate(FORCED):
                state[slot, 0, f * LEV + l] += forced[N_FORCED + i]
                state[slot, 1, f * LEV + l] += forced_y[N_FORCED + i]

    wait(send.at[pl.ds(0, n_tx - 1)], send_sem, R_ROUTE)
    wait(ice_v.at[0], send_sem, R_ICE)
    wait(stat, send_sem, R_STAT_Y)
    wait(stat_ye, send_sem, R_STAT_YE)
    wait(forced_ye, send_sem, R_FORCED_YE)
    wait(stat_x, send_sem, R_STAT_X)
    wait(forced, send_sem, R_FORCED_Y)
    wait(forced_x.at[pl.ds(0, 3)], send_sem, R_FORCED_LEFT)

    @pl.when(jnp.logical_not(at_last))
    def _():
        wait(forced_x.at[pl.ds(0, 3)], send_sem, R_FORCED_RIGHT)

    @pl.when(at_first)
    def _():
        wait(forced_x.at[pl.ds(0, 2)], send_sem, R_FORCED_RIGHT)

    @pl.when(grp == 1)
    def _():
        wait(send.at[pl.ds(0, 2)], send_sem, R_BORDER)

    @pl.when(z == half - 1)
    def _():
        wait(border_ice.at[0], send_sem, R_BORDER_ICE)

    @pl.when(at_last)
    def _():
        wait(border_land, send_sem, R_BORDER_LAND)


def per_device(sizes, innov, weight, level, tile, cell, land, hdiff, vdiff, coupling, ice):
    scratch = [
        pltpu.VMEM((ITERS * PROFS * VARS, DEPTH), F32),
        pltpu.VMEM((ITERS, PROFS, DEPTH), F32),
        pltpu.VMEM((ITERS, PROFS, DEPTH), jnp.int32),
        pltpu.VMEM((ITERS, PROFS), jnp.int32),
        pltpu.VMEM((ITERS, PROFS), jnp.int32),
        pltpu.VMEM((ROWS, LANES), jnp.int32),
        pltpu.VMEM((F, F), F32),
        pltpu.VMEM((2, ITERS, ICEV, 4, LANES), F32),
        pltpu.VMEM((N_STATIC, ROWS, LANES), F32),
        pltpu.VMEM((N_STATIC, ROWS, LANES), F32),
        pltpu.VMEM((2, ROWS, LANES), F32),
        pltpu.VMEM((6, ROWS, LANES), F32),
        pltpu.VMEM((SLOTS, MESSAGE, LANES), F32),
        pltpu.VMEM((SLOTS, MESSAGE, LANES), F32),
        pltpu.VMEM((ITERS * N_FORCED, ROWS, LANES), F32),
        pltpu.VMEM((ITERS * N_FORCED, ROWS, LANES), F32),
        pltpu.VMEM((2, ITERS, ROWS, LANES), F32),
        pltpu.VMEM((6, ITERS, ROWS, LANES), F32),
        pltpu.VMEM((2, ROWS, LANES), F32),
        pltpu.VMEM((2, ITERS, ROWS, LANES), F32),
        pltpu.VMEM((SLOTS, MESSAGE, LANES), F32),
        pltpu.VMEM((2, ITERS, ICEV, 4, LANES), F32),
        pltpu.VMEM((ROWS, LANES), F32),
        pltpu.VMEM((ITERS, ROWS, LANES), F32),
        pltpu.VMEM((2, 2, F * LEV, ROWS, LANES), F32),
        pltpu.SemaphoreType.DMA((N_LOCAL,)),
        pltpu.SemaphoreType.DMA((N_REMOTE,)),
        pltpu.SemaphoreType.DMA((N_REMOTE,)),
        pltpu.SemaphoreType.REGULAR((GROUPS + 2,)),
    ]
    operands = (
        innov.reshape(ITERS * PROFS * VARS, DEPTH),
        weight,
        level,
        tile.reshape(ITERS, PROFS),
        cell,
        land,
        hdiff,
        vdiff,
        coupling,
        ice,
    )
    anywhere = pl.BlockSpec(memory_space=pltpu.HBM)
    return pl.pallas_call(
        functools.partial(kernel, sizes),
        out_shape=jax.ShapeDtypeStruct((F, LEV, ROWS, LANES), F32),
        in_specs=[anywhere] * len(operands),
        out_specs=pl.BlockSpec(memory_space=pltpu.VMEM),
        scratch_shapes=scratch,
        compiler_params=pltpu.CompilerParams(
            collective_id=0, has_side_effects=True, vmem_limit_bytes=16 * 1024 * 1024
        ),
    )(*(pltpu.with_memory_space_constraint(operand, pltpu.HBM) for operand in operands))


def solution(mesh):
    sizes = tuple(mesh.shape[axis] for axis in ("ty", "tx", "grp"))
    in_specs = (
        P(None, ("ty", "tx", "grp"), None, None),
        P(None, ("ty", "tx", "grp"), None),
        P(None, ("ty", "tx", "grp"), None),
        P(None, ("ty", "tx", "grp"), None),
        P(None, ("ty", "tx", "grp")),
        P("ty", ("tx", "grp")),
        P("ty", ("tx", "grp")),
        P(None, "ty", ("tx", "grp")),
        P(),
        P(None, None, ("ty", "grp"), "tx"),
    )
    out_specs = P(None, None, "ty", ("tx", "grp"))
    return jax.shard_map(
        functools.partial(per_device, sizes), mesh=mesh, in_specs=in_specs, out_specs=out_specs, check_vma=False
    )
```

```python
import functools

import jax
import jax.numpy as jnp
from jax import lax
from jax.experimental import pallas as pl
from jax.experimental.pallas import tpu as pltpu
from jax.sharding import PartitionSpec as P

F = 5
LEV = 8
VARS = 2
ICEV = 4
ROWS = 8
LANES = 128
DEPTH = 128
PROFS = 128
ITERS = 2
SUB = 2
SLOTS = 32
N_FORCED = VARS * LEV + (ICEV - VARS)
N_STATIC = LEV + 2
MESH = pl.DeviceIdType.MESH
F32 = jnp.float32
BF16 = jnp.bfloat16
NT = (((1,), (1,)), ((), ()))

FORCED = [(f, l) for f in range(VARS) for l in range(LEV)] + [(f, 0) for f in range(VARS, ICEV)]

L_LEVEL, L_WEIGHT, L_INNOV, L_TILE, L_CELL, L_LAND, L_HDIFF, L_VDIFF, L_ICE, L_COUPLING, L_OWN, L_BORDER = range(12)
N_LOCAL = 12
R_ROUTE, R_ICE, R_STAT_Y, R_STAT_X, R_FORCED_Y, R_FORCED_RIGHT, R_FORCED_LEFT = range(7)
R_BORDER, R_BORDER_ICE, R_BORDER_LAND, R_STAT_YE, R_FORCED_YE = range(7, 12)
N_REMOTE = 12
GROUPS = 3
S_NEAR, S_BESIDE, S_DIAGONAL = GROUPS, GROUPS + 1, GROUPS + 2

RANK_ROWS = 4
RANKS = 4
MESSAGE = RANK_ROWS + 1


def iota(shape, axis):
    return lax.broadcasted_iota(jnp.int32, shape, axis)


def split(x):
    high = x.astype(BF16)
    low = (x - high.astype(F32)).astype(BF16)
    return high, low


def roll_lanes(x, shift):
    shift %= LANES
    return x if shift == 0 else pltpu.roll(x, shift, 1)


def dot_nt(a, b):
    return lax.dot_general(a, b, NT, preferred_element_type=F32)


def level_sums(weight, level, innovs):
    level_t = level.T
    out = []
    for innov in innovs:
        weighted_t = (weight * innov).T
        rows = [
            jnp.sum(jnp.where(level_t == l, weighted_t, 0.0), axis=0, keepdims=True) for l in range(LEV)
        ]
        out.append(jnp.concatenate(rows, axis=0))
    return out


def rank_in_tile(tile):
    named = (tile == iota((SLOTS, PROFS), 0)).astype(F32)
    before = (iota((PROFS, PROFS), 0) < iota((PROFS, PROFS), 1)).astype(F32).astype(BF16)
    counts = lax.dot_general(
        named.astype(BF16), before, (((1,), (0,)), ((), ())), preferred_element_type=F32
    )
    return named.astype(BF16), jnp.sum(named * counts, axis=0, keepdims=True).astype(jnp.int32)


def pack_messages(columns, tiles, cells):
    row = iota((8, PROFS), 0)
    zero = jnp.zeros((8, PROFS), F32)
    named, ranks, tops, rests, yx = [], [], [], [], []
    for w in range(ITERS):
        n, rank = rank_in_tile(tiles[w])
        named += [n, n]
        ranks.append(rank)
        top = [c.astype(BF16).astype(F32) for c in columns[w]]
        tops.append(top)
        rests.append([c - t for c, t in zip(columns[w], top)])
        cell = cells[w]
        yx.append(jnp.where(row % 2 == 0, (cell // LANES).astype(F32), (cell % LANES).astype(F32)))
    high = [[], []]
    low = [[], []]

    def add(w, top, rest):
        for u in range(ITERS):
            high[u].append(top if u == w else zero)
            low[u].append(rest if u == w else zero)

    for upper in range(RANK_ROWS):
        for w in range(ITERS):
            for v in range(VARS):
                for r in range(RANKS):
                    here = ranks[w] == upper * RANKS + r
                    add(w, jnp.where(here, tops[w][v], 0.0), jnp.where(here, rests[w][v], 0.0))
    for upper in range(RANK_ROWS):
        for w in range(ITERS):
            add(w, jnp.where(ranks[w] == upper * RANKS + row // 2, yx[w], 0.0), zero)
        add(0, zero, zero)
        add(0, zero, zero)
    values = jnp.concatenate(
        [jnp.concatenate(part[w], axis=0).astype(BF16) for w in range(ITERS) for part in (high, low)], axis=1
    )
    return dot_nt(jnp.concatenate(named, axis=1), values)


def gather_cells(received):
    got = jnp.concatenate([received(j) for j in range(RANK_ROWS)], axis=0).T
    cells = received(RANK_ROWS)
    where_ = jnp.concatenate([roll_lanes(cells, -32 * j) for j in range(RANK_ROWS)], axis=0).T
    top = got.astype(BF16).astype(F32)
    rest = got - top
    y_of_row = iota((ROWS, LANES), 0).astype(F32)
    x_of_row = iota((LANES, LANES), 0).astype(F32)
    out = []
    for w in range(ITERS):
        left, right = [], []
        for r in range(RANKS):
            at = (w * RANKS + r) * 2
            y_here = where_[at : at + 1] == y_of_row
            x_here = (where_[at + 1 : at + 2] == x_of_row).astype(F32).astype(BF16)
            for part in (top, rest):
                blocks = []
                for v in range(VARS):
                    for l in range(LEV):
                        at = w * 64 + v * 32 + r * LEV + l
                        blocks.append(jnp.where(y_here, part[at : at + 1], 0.0))
                left.append(jnp.concatenate(blocks, axis=0).astype(BF16))
                right.append(x_here)
        out.append(dot_nt(jnp.concatenate(left, axis=1), jnp.concatenate(right, axis=1)))
    return out


def gather_edges(received, firsts):
    got = jnp.concatenate([received(j) for j in range(RANK_ROWS)], axis=0).T
    cells = received(RANK_ROWS)
    where_ = jnp.concatenate([roll_lanes(cells, -32 * j) for j in range(RANK_ROWS)], axis=0).T
    top = got.astype(BF16).astype(F32)
    rest = got - top
    row = iota((ROWS, LANES), 0)
    y_of_row = row.astype(F32)
    zero = jnp.zeros((ROWS, LANES), F32)
    out = []
    for w in range(ITERS):
        left, right = [], []
        for r in range(RANKS):
            at = (w * RANKS + r) * 2
            y_here = (where_[at : at + 1] == y_of_row).astype(F32)
            x_here = [where_[at + 1 : at + 2] == (first + row % 4).astype(F32) for first in firsts]
            for part in (top, rest):
                blocks = [[] for _ in firsts]
                for l in range(LEV):
                    at = w * 64 + r * LEV + l
                    both = jnp.where(row < 4, part[at : at + 1], part[at + 32 : at + 33])
                    for block, here in zip(blocks, x_here):
                        block += [jnp.where(here, both, 0.0), zero]
                left.append(y_here)
                right.append(jnp.concatenate(sum(blocks, []), axis=0).astype(BF16))
        sums = dot_nt(jnp.concatenate(left, axis=1).astype(BF16), jnp.concatenate(right, axis=1))
        out.append([sums[:, i * LANES : (i + 1) * LANES] for i in range(len(firsts))])
    return out


def edge_ocean(ocean, first):
    lane = iota((ROWS, LANES), 1)
    out = jnp.where(lane < 4, roll_lanes(ocean, -first), 0.0)
    for width in (4, 8, 16, 32, 64):
        out = out + roll_lanes(out, width)
    return out


def edge_melt(melts, first):
    lane = iota((ROWS, LANES), 1)
    out = jnp.zeros((ROWS, LANES), F32)
    for f, melt in enumerate(melts):
        here = jnp.logical_and(lane >= 4 * f, lane < 4 * f + 4)
        out = jnp.where(here, roll_lanes(melt, 4 * f - first), out)
    return out


def pack_edges(items):
    lane = iota((ROWS, LANES), 1)
    last = jnp.zeros((ROWS, LANES), F32)
    first = jnp.zeros((ROWS, LANES), F32)
    for slot, level, rows in items:
        at = 16 * level + 4 * slot
        turned = roll_lanes(rows, at + 4)
        last = jnp.where(jnp.logical_and(lane >= at, lane < at + 4), turned, last)
        first = jnp.where(jnp.logical_and(lane >= at + 4, lane < at + 8), turned, first)
    return last, first


def strip(slot, from_left, own_last, own_first, from_right):
    group = iota((ROWS, LANES), 1) % 16
    low = jnp.where(group < 4, roll_lanes(from_left, -4 * slot), roll_lanes(own_first, -4 * slot))
    high = jnp.where(group < 12, roll_lanes(own_last, 8 - 4 * slot), roll_lanes(from_right, 8 - 4 * slot))
    return jnp.where(group < 8, low, high)


def strips(slots, received, own):
    upper = iota((ROWS, LANES), 0) < 4
    left_halo = jnp.where(upper, received[1], received[2])
    right_halo = jnp.where(upper, received[4], received[5])
    sides = ((received[0], received[3]), (left_halo, right_halo))
    return [
        tuple(strip(slot, sides[t][0], own[t][0], own[t][1], sides[t][1]) for t in range(2)) for slot in slots
    ]


def y_neighbours(pair):
    row = iota((ROWS, LANES), 0)
    a, b = pair
    next_a, next_b = pltpu.roll(a, ROWS - 1, 0), pltpu.roll(b, ROWS - 1, 0)
    prev_a, prev_b = pltpu.roll(a, 1, 0), pltpu.roll(b, 1, 0)
    plus = (jnp.where(row == ROWS - 1, next_b, next_a), jnp.where(row == ROWS - 1, next_a, next_b))
    minus = (jnp.where(row == 0, prev_b, prev_a), jnp.where(row == 0, prev_a, prev_b))
    return plus, minus


def edge_pair(one):
    group = iota((ROWS, LANES), 1) % 16
    return jnp.where(group == 13, roll_lanes(one, 10), one)


def x_neighbours(one, edges, level):
    lane = iota((ROWS, LANES), 1)
    halo = roll_lanes(edges, LANES - 1 - 12 - 16 * level)
    plus = jnp.where(lane == LANES - 1, halo, roll_lanes(one, -1))
    minus = jnp.where(lane == 0, halo, roll_lanes(one, 1))
    return plus, minus


def strip_x_neighbours(one):
    return roll_lanes(one, -1), roll_lanes(one, 1)


def weights_of(diff, ocean, x_pairs):
    (diff_n, ocean_n) = (y_neighbours(diff), y_neighbours(ocean))
    out = []
    for t in range(2):
        near = [(diff_n[0][t], ocean_n[0][t]), (diff_n[1][t], ocean_n[1][t])] + list(x_pairs[t])
        faces = [0.5 * (diff[t] + d) * ocean[t] * o for d, o in near]
        out.append((1.0 - (faces[0] + faces[1] + faces[2] + faces[3]), faces))
    return out


def lateral(one, near, weights):
    centre, faces = weights
    total = centre * one
    for face, value in zip(faces, near):
        total = total + face * value
    return total


def couple(diffused, coef, ocean):
    out = []
    for f in range(F):
        total = None
        for g in range(F):
            if diffused[g] is not None:
                term = coef[g][f] * diffused[g]
                total = term if total is None else total + term
        out.append(ocean * total)
    return out


def step_strips(old, weights, vertical, ocean, coef):
    lane = iota((ROWS, LANES), 1)
    diffused = [[None] * F, [None] * F]
    for f in range(F):
        if old[f] is None:
            continue
        plus, minus = y_neighbours(old[f])
        for t in range(2):
            one = old[f][t]
            x_plus, x_minus = strip_x_neighbours(one)
            below = jnp.where(lane < LANES - 16, roll_lanes(one, -16), 0.0)
            flux = vertical[t] * (below - one)
            above = jnp.where(lane < 16, 0.0, roll_lanes(flux, 16))
            diffused[t][f] = lateral(one, (plus[t], minus[t], x_plus, x_minus), weights[t]) + (flux - above)
    coupled = [couple(diffused[t], coef, ocean[t]) for t in range(2)]
    return [(coupled[0][f], coupled[1][f]) for f in range(F)]


def step_tile(read, write, live, edges, weights, vertical, ocean, coef, tiles):
    above = [[None] * F, [None] * F]
    for l in range(LEV):
        diffused = [[None] * F, [None] * F]
        for f in range(F):
            here = read(f, l) if (f, l) in live else None
            below = read(f, l + 1) if (f, l + 1) in live else None
            near = y_neighbours(here) if here is not None else None
            for t in range(tiles):
                flux = None
                if here is not None and below is not None:
                    flux = vertical(l, t) * (below[t] - here[t])
                elif here is not None:
                    flux = -(vertical(l, t) * here[t])
                elif below is not None:
                    flux = vertical(l, t) * below[t]
                total = None
                if here is not None:
                    x_plus, x_minus = x_neighbours(here[t], edges[f][t], l)
                    total = lateral(here[t], (near[0][t], near[1][t], x_plus, x_minus), weights[t])
                if flux is not None:
                    total = flux if total is None else total + flux
                if above[t][f] is not None:
                    total = -above[t][f] if total is None else total - above[t][f]
                above[t][f] = flux
                diffused[t][f] = total
        for t in range(tiles):
            for f, value in enumerate(couple(diffused[t], coef, ocean[t])):
                write(f, l, t, value)


def kernel(
    sizes,
    innov,
    weight,
    level,
    tile,
    cell,
    land,
    hdiff,
    vdiff,
    coupling,
    ice,
    out,
    innov_v,
    weight_v,
    level_v,
    tile_v,
    cell_v,
    land_v,
    coupling_v,
    ice_v,
    stat,
    stat_y,
    stat_e,
    stat_x,
    send,
    recv,
    forced,
    forced_y,
    forced_e,
    forced_x,
    stat_ye,
    forced_ye,
    border,
    border_edge,
    border_ice,
    border_land,
    border_e,
    state,
    local_sem,
    send_sem,
    recv_sem,
    enter_sem,
):
    n_ty, n_tx, n_grp = sizes
    ty, tx, grp = lax.axis_index("ty"), lax.axis_index("tx"), lax.axis_index("grp")
    blocks = n_tx * n_grp
    block = tx * n_grp + grp
    right, left = (block + 1) % blocks, (block + blocks - 1) % blocks
    down, up = (ty + 1) % n_ty, (ty + n_ty - 1) % n_ty

    def at(row, column):
        return (row, column // n_grp, column % n_grp)

    half = n_tx // 2
    z, side = tx % half, tx // half
    at_first = jnp.logical_and(z == 0, grp == 1)
    at_last = jnp.logical_and(z == half - 1, grp == 1)

    def fetch(src, dst, sem):
        copy = pltpu.make_async_copy(src, dst, local_sem.at[sem])
        copy.start()
        return copy

    def put(src, dst, sem, device):
        pltpu.make_async_remote_copy(
            src_ref=src,
            dst_ref=dst,
            send_sem=send_sem.at[sem],
            recv_sem=recv_sem.at[sem],
            device_id=device,
            device_id_type=MESH,
        ).start()

    def wait(ref, sems, sem):
        pltpu.make_async_copy(ref, ref, sems.at[sem]).wait()

    def signal(sem, device):
        pl.semaphore_signal(sem, inc=1, device_id=device, device_id_type=MESH)

    def peers(low, high, act):
        def one(i, carry):
            for half_of in range(2):
                act(i + half_of * half)
            return carry

        lax.fori_loop(low, high, one, 0)

    def turn_y(row):
        chip, chips = row // 2, n_ty // 2
        return 2 * jnp.where(chip < chips // 2, chip, chips + chips // 2 - 1 - chip) + 1 - row % 2

    partner = (ty, tx, 1 - grp)
    nearest = [
        (at(down, block), turn_y(down) > turn_y(ty)),
        (at(up, block), turn_y(up) > turn_y(ty)),
        (partner, grp == 0),
    ]
    bounds = [0, half // 4, half // 2, half]
    group = jnp.where(z >= bounds[1], 1, 0) + jnp.where(z >= bounds[2], 1, 0)

    if n_tx < SLOTS:
        recv[...] = jnp.zeros(recv.shape, F32)
        border[...] = jnp.zeros(border.shape, F32)

    barrier = pltpu.get_barrier_semaphore()
    for device, after in nearest:
        pl.when(after)(functools.partial(signal, barrier, device))

    @pl.when(side == 0)
    def _():
        signal(barrier, (ty, tx + half, grp))

    peers(z + 1, half, lambda peer: signal(barrier, (ty, peer, grp)))

    at_border = jnp.logical_and(z == 0, grp == 0)

    @pl.when(at_border)
    def _():
        signal(barrier, (ty, (tx + n_tx - 1) % n_tx, 1))

    @pl.when(at_first)
    def _():
        signal(barrier, (ty, (tx + n_tx - 1) % n_tx, 0))

    earlier = 2 * z + side + jnp.where(z == half - 1, 1, 0)
    later_near = 0
    for _, after in nearest:
        earlier = earlier + jnp.where(after, 0, 1)
        later_near = later_near + jnp.where(after, 1, 0)

    def await_signals(sem, count):
        @pl.when(count > 0)
        def _():
            pl.semaphore_wait(sem, count)

    loads = [
        fetch(level, level_v, L_LEVEL),
        fetch(weight, weight_v, L_WEIGHT),
        fetch(innov, innov_v, L_INNOV),
        fetch(tile, tile_v, L_TILE),
        fetch(cell, cell_v, L_CELL),
    ]
    ice_here = ice.at[:, :, :, pl.ds(pl.multiple_of(grp * LANES, LANES), LANES)]
    ice_there = ice.at[:, :, :, pl.ds(pl.multiple_of((1 - grp) * LANES, LANES), LANES)]
    ice_last = ice.at[:, :, :, pl.ds((n_grp - 1) * LANES, LANES)]
    static_loads = [
        fetch(land, land_v, L_LAND),
        fetch(hdiff, stat.at[LEV], L_HDIFF),
        fetch(vdiff, stat.at[pl.ds(0, LEV)], L_VDIFF),
        fetch(ice_here, ice_v.at[grp], L_ICE),
        fetch(coupling, coupling_v, L_COUPLING),
    ]

    for load in loads:
        load.wait()
    columns = [
        level_sums(
            weight_v[w],
            level_v[w],
            [innov_v[pl.ds(w * PROFS * VARS + v, PROFS, stride=VARS), :] for v in range(VARS)],
        )
        for w in range(ITERS)
    ]
    messages = pack_messages(
        columns, [tile_v[pl.ds(w, 1), :] for w in range(ITERS)], [cell_v[pl.ds(w, 1), :] for w in range(ITERS)]
    )
    for j in range(MESSAGE):
        send[:, j, :] = messages[:, j * LANES : (j + 1) * LANES]

    await_signals(barrier, earlier)
    for load in static_loads:
        load.wait()
    ocean_tile = land_v[...].astype(F32)
    stat[LEV + 1] = ocean_tile

    @pl.when(z == half - 1)
    def _():
        put(ice_last, border_ice.at[grp], R_BORDER_ICE, (ty, (tx + 1) % n_tx, 1))

    @pl.when(at_last)
    def _():
        put(stat.at[LEV + 1], border_land, R_BORDER_LAND, (ty, (tx + 1) % n_tx, 1))

    for device, after in nearest:
        pl.when(jnp.logical_not(after))(functools.partial(signal, enter_sem.at[S_NEAR], device))

    @pl.when(jnp.logical_and(grp == 1, z > 0))
    def _():
        signal(enter_sem.at[S_BESIDE], (ty, tx - 1, 1))

    def route(peer):
        put(send.at[peer], recv.at[tx], R_ROUTE, (ty, peer, grp))

    def route_border(first_tx):
        put(send.at[(first_tx + n_tx - 1) % n_tx], border.at[tx], R_BORDER, (ty, first_tx, 1))

    @pl.when(jnp.logical_and(grp == 1, z > 0))
    def _():
        route_border(0)
        route_border(half)

    @pl.when(jnp.logical_and(at_first, side == 1))
    def _():
        route_border(0)

    peers(0, z, route)

    @pl.when(side == 1)
    def _():
        route(tx - half)

    peers(0, z, lambda peer: signal(enter_sem.at[group], (ty, peer, grp)))

    @pl.when(side == 1)
    def _():
        signal(enter_sem.at[group], (ty, tx - half, grp))

    own = fetch(send.at[tx], recv.at[tx], L_OWN)

    @pl.when(at_first)
    def _():
        pltpu.make_async_copy(
            send.at[(tx + n_tx - 1) % n_tx], border.at[tx], local_sem.at[L_BORDER]
        ).start()

    def static_items(ref):
        items = [(0, l, ref[l]) for l in range(LEV)]
        return items + [(1 + j, l, ref[LEV + j]) for j in range(2) for l in range(LEV)]

    last, first = pack_edges(static_items(stat))
    stat_e[0] = last
    stat_e[1] = first

    def route_later(g):
        low, high = bounds[g], bounds[g + 1]
        start = jnp.maximum(z + 1, low)
        twin = jnp.logical_and(side == 0, group == g)
        await_signals(enter_sem.at[g], 2 * jnp.maximum(high - start, 0) + jnp.where(twin, 1, 0))
        peers(start, high, route)

        @pl.when(twin)
        def _():
            route(tx + half)
            pl.when(at_first)(functools.partial(route_border, half))

    for g in range(GROUPS - 1):
        route_later(g)
    await_signals(enter_sem.at[S_NEAR], later_near)
    for r in (up, down):
        signal(enter_sem.at[S_DIAGONAL], at(r, block))
    put(ice_there, ice_v.at[grp], R_ICE, partner)

    def tell():
        signal(enter_sem.at[S_BESIDE], (ty, (tx + 1) % n_tx, 0))

    soon = jnp.logical_or(z + 1 < bounds[GROUPS - 1], z == half - 1)
    pl.when(jnp.logical_and(grp == 0, soon))(tell)
    route_later(GROUPS - 1)
    pl.when(jnp.logical_and(grp == 0, jnp.logical_not(soon)))(tell)
    def exchange_y(rows, rows_y, sem):
        for r, part in ((up, pl.ds(0, 4)), (down, pl.ds(4, 4))):
            whole_ = (slice(None),) * (len(rows.shape) - 2)
            put(rows.at[*whole_, part], rows_y.at[*whole_, part], sem, at(r, block))

    def exchange_x(edge, column, rows, rows_x, sem):
        for slot, r in reversed(list(enumerate((ty, up, down)))):
            put(rows.at[edge], rows_x.at[edge * 3 + slot], sem, at(r, column))

    beside = jnp.where(grp == 0, left, right)

    def meet_beside():
        await_signals(enter_sem.at[S_BESIDE], jnp.where(jnp.logical_or(grp == 0, z < half - 1), 1, 0))
        for r in (up, down):
            signal(enter_sem.at[S_DIAGONAL + 1], at(r, block))
        pl.semaphore_wait(enter_sem.at[S_DIAGONAL + 1], 2)
        exchange_x(1 - grp, beside, stat_e, stat_x, R_STAT_X)

    def force_beside():
        @pl.when(jnp.logical_not(at_last))
        def _():
            exchange_x(1 - grp, beside, forced_e, forced_x, R_FORCED_RIGHT + 1 - grp)

    pl.semaphore_wait(enter_sem.at[S_DIAGONAL], 2)
    exchange_y(stat, stat_y, R_STAT_Y)
    exchange_y(stat_e, stat_ye, R_STAT_YE)
    exchange_x(grp, tx * n_grp + 1 - grp, stat_e, stat_x, R_STAT_X)
    pl.when(jnp.logical_not(at_border))(meet_beside)

    def melts_of(ref, w):
        return [jnp.concatenate([ref[0, w, f], ref[1, w, f]], axis=0) for f in range(ICEV)]

    last_cols, first_cols = LANES - 4, 0
    wait(ice_v.at[0], recv_sem, R_ICE)
    melts = [melts_of(ice_v, w) for w in range(ITERS)]
    oceans_e = [edge_ocean(ocean_tile, first) for first in (last_cols, first_cols)]
    melts_e = [[edge_melt(melts[w], first) for first in (last_cols, first_cols)] for w in range(ITERS)]

    @pl.when(at_first)
    def _():
        wait(border_land, recv_sem, R_BORDER_LAND)
        wait(border_ice, recv_sem, R_BORDER_ICE)
        border_edge[0] = edge_ocean(border_land[...], last_cols)
        for w in range(ITERS):
            border_edge[1 + w] = edge_melt(melts_of(border_ice, w), last_cols)

    own.wait()
    wait(recv.at[pl.ds(0, n_tx - 1)], recv_sem, R_ROUTE)
    sums_e = gather_edges(lambda j: recv[:, j, :], (last_cols, first_cols))
    for w in range(ITERS):
        last, first = [oceans_e[i] * (sums_e[w][i] + melts_e[w][i]) for i in range(2)]
        forced_e[0, w] = last
        forced_e[1, w] = roll_lanes(first, 4)

    pl.when(jnp.logical_not(at_border))(force_beside)
    exchange_x(grp, tx * n_grp + 1 - grp, forced_e, forced_x, R_FORCED_RIGHT + grp)
    exchange_y(forced_e, forced_ye, R_FORCED_YE)

    @pl.when(at_first)
    def _():
        wait(border.at[tx], local_sem, L_BORDER)
        wait(border.at[pl.ds(0, n_tx - 1)], recv_sem, R_BORDER)
        sums_b = gather_edges(lambda j: border[:, j, :], (last_cols,))
        for w in range(ITERS):
            border_e[w] = border_edge[0] * (sums_b[w][0] + border_edge[1 + w])
        for slot, r in ((1, up), (2, down), (0, ty)):
            put(border_e, forced_x.at[slot], R_FORCED_RIGHT, (r, tx, 0))

    sums = gather_cells(lambda j: recv[:, j, :])
    for w in range(ITERS):
        for i, (f, l) in enumerate(FORCED):
            value = sums[w][i * ROWS : (i + 1) * ROWS] if f < VARS else None
            if l == 0:
                value = melts[w][f] if value is None else value + melts[w][f]
            forced[w * N_FORCED + i] = ocean_tile * value
    exchange_y(forced, forced_y, R_FORCED_Y)

    @pl.when(at_border)
    def _():
        meet_beside()
        force_beside()


    wait(stat_y, recv_sem, R_STAT_Y)
    wait(stat_ye, recv_sem, R_STAT_YE)
    wait(stat_x, recv_sem, R_STAT_X)
    own_edges = ((stat_e[0], stat_e[1]), (stat_ye[0], stat_ye[1]))
    vertical_s, diff_s, ocean_s = strips((0, 1, 2), [stat_x[i] for i in range(6)], own_edges)
    diff = (stat[LEV], stat_y[LEV])
    ocean = (stat[LEV + 1], stat_y[LEV + 1])
    x_pairs, x_pairs_s = [], []
    for t in range(2):
        d = x_neighbours(diff[t], edge_pair(diff_s[t]), 0)
        o = x_neighbours(ocean[t], edge_pair(ocean_s[t]), 0)
        x_pairs.append(((d[0], o[0]), (d[1], o[1])))
        d, o = strip_x_neighbours(diff_s[t]), strip_x_neighbours(ocean_s[t])
        x_pairs_s.append(((d[0], o[0]), (d[1], o[1])))
    weights = weights_of(diff, ocean, x_pairs)
    weights_s = weights_of(diff_s, ocean_s, x_pairs_s)
    coef = [
        [
            jnp.broadcast_to(coupling_v[g : g + 1, f : f + 1], (ROWS, LANES)) + (1.0 if f == g else 0.0)
            for f in range(F)
        ]
        for g in range(F)
    ]

    def vertical(l, t):
        return stat[l] if t == 0 else stat_y[l]

    wait(forced_y, recv_sem, R_FORCED_Y)
    wait(forced_ye, recv_sem, R_FORCED_YE)
    wait(forced_x.at[pl.ds(3, 3)], recv_sem, R_FORCED_LEFT)
    wait(forced_x.at[pl.ds(0, 3)], recv_sem, R_FORCED_RIGHT)

    def forced_strips(w):
        own_edges = ((forced_e[0, w], forced_e[1, w]), (forced_ye[0, w], forced_ye[1, w]))
        return strips(range(ICEV), [forced_x[i, w] for i in range(6)], own_edges)

    index = {item: i for i, item in enumerate(FORCED)}
    whole = {(f, l) for f in range(F) for l in range(LEV)}
    packed = forced_strips(0) + [None]

    def read_forced(f, l):
        return forced[index[f, l]], forced_y[index[f, l]]

    def reader(slot):
        return lambda f, l: (state[slot, 0, f * LEV + l], state[slot, 1, f * LEV + l])

    def writer(slot):
        def write(f, l, t, value):
            state[slot, t, f * LEV + l] = value

        return write

    def write_out(f, l, t, value):
        out[f, l] = value

    n_steps = ITERS * SUB
    for step in range(n_steps):
        end = step == n_steps - 1
        edges = [None if p is None else (edge_pair(p[0]), edge_pair(p[1])) for p in packed]
        step_tile(
            read_forced if step == 0 else reader(step % 2),
            write_out if end else writer((step + 1) % 2),
            set(FORCED) if step == 0 else whole,
            edges,
            weights,
            vertical,
            ocean,
            coef,
            1 if end else 2,
        )
        if not end:
            packed = step_strips(packed, weights_s, vertical_s, ocean_s, coef)
        if step == SUB - 1:
            slot = (step + 1) % 2
            added = forced_strips(1)
            for f in range(ICEV):
                packed[f] = tuple(packed[f][t] + added[f][t] for t in range(2))
            for i, (f, l) in enumerate(FORCED):
                state[slot, 0, f * LEV + l] += forced[N_FORCED + i]
                state[slot, 1, f * LEV + l] += forced_y[N_FORCED + i]

    wait(send.at[pl.ds(0, n_tx - 1)], send_sem, R_ROUTE)
    wait(ice_v.at[0], send_sem, R_ICE)
    wait(stat, send_sem, R_STAT_Y)
    wait(stat_ye, send_sem, R_STAT_YE)
    wait(forced_ye, send_sem, R_FORCED_YE)
    wait(stat_x, send_sem, R_STAT_X)
    wait(forced, send_sem, R_FORCED_Y)
    wait(forced_x.at[pl.ds(0, 3)], send_sem, R_FORCED_LEFT)

    @pl.when(jnp.logical_not(at_last))
    def _():
        wait(forced_x.at[pl.ds(0, 3)], send_sem, R_FORCED_RIGHT)

    @pl.when(at_first)
    def _():
        wait(forced_x.at[pl.ds(0, 3)], send_sem, R_FORCED_RIGHT)

    @pl.when(grp == 1)
    def _():
        wait(send.at[0], send_sem, R_BORDER)

        @pl.when(z > 0)
        def _():
            wait(send.at[0], send_sem, R_BORDER)

    @pl.when(z == half - 1)
    def _():
        wait(border_ice.at[0], send_sem, R_BORDER_ICE)

    @pl.when(at_last)
    def _():
        wait(border_land, send_sem, R_BORDER_LAND)


def per_device(sizes, innov, weight, level, tile, cell, land, hdiff, vdiff, coupling, ice):
    scratch = [
        pltpu.VMEM((ITERS * PROFS * VARS, DEPTH), F32),
        pltpu.VMEM((ITERS, PROFS, DEPTH), F32),
        pltpu.VMEM((ITERS, PROFS, DEPTH), jnp.int32),
        pltpu.VMEM((ITERS, PROFS), jnp.int32),
        pltpu.VMEM((ITERS, PROFS), jnp.int32),
        pltpu.VMEM((ROWS, LANES), jnp.int32),
        pltpu.VMEM((F, F), F32),
        pltpu.VMEM((2, ITERS, ICEV, 4, LANES), F32),
        pltpu.VMEM((N_STATIC, ROWS, LANES), F32),
        pltpu.VMEM((N_STATIC, ROWS, LANES), F32),
        pltpu.VMEM((2, ROWS, LANES), F32),
        pltpu.VMEM((6, ROWS, LANES), F32),
        pltpu.VMEM((SLOTS, MESSAGE, LANES), F32),
        pltpu.VMEM((SLOTS, MESSAGE, LANES), F32),
        pltpu.VMEM((ITERS * N_FORCED, ROWS, LANES), F32),
        pltpu.VMEM((ITERS * N_FORCED, ROWS, LANES), F32),
        pltpu.VMEM((2, ITERS, ROWS, LANES), F32),
        pltpu.VMEM((6, ITERS, ROWS, LANES), F32),
        pltpu.VMEM((2, ROWS, LANES), F32),
        pltpu.VMEM((2, ITERS, ROWS, LANES), F32),
        pltpu.VMEM((SLOTS, MESSAGE, LANES), F32),
        pltpu.VMEM((1 + ITERS, ROWS, LANES), F32),
        pltpu.VMEM((2, ITERS, ICEV, 4, LANES), F32),
        pltpu.VMEM((ROWS, LANES), F32),
        pltpu.VMEM((ITERS, ROWS, LANES), F32),
        pltpu.VMEM((2, 2, F * LEV, ROWS, LANES), F32),
        pltpu.SemaphoreType.DMA((N_LOCAL,)),
        pltpu.SemaphoreType.DMA((N_REMOTE,)),
        pltpu.SemaphoreType.DMA((N_REMOTE,)),
        pltpu.SemaphoreType.REGULAR((GROUPS + 4,)),
    ]
    operands = (
        innov.reshape(ITERS * PROFS * VARS, DEPTH),
        weight,
        level,
        tile.reshape(ITERS, PROFS),
        cell,
        land,
        hdiff,
        vdiff,
        coupling,
        ice,
    )
    anywhere = pl.BlockSpec(memory_space=pltpu.HBM)
    return pl.pallas_call(
        functools.partial(kernel, sizes),
        out_shape=jax.ShapeDtypeStruct((F, LEV, ROWS, LANES), F32),
        in_specs=[anywhere] * len(operands),
        out_specs=pl.BlockSpec(memory_space=pltpu.VMEM),
        scratch_shapes=scratch,
        compiler_params=pltpu.CompilerParams(
            collective_id=0, has_side_effects=True, vmem_limit_bytes=16 * 1024 * 1024
        ),
    )(*(pltpu.with_memory_space_constraint(operand, pltpu.HBM) for operand in operands))


def solution(mesh):
    sizes = tuple(mesh.shape[axis] for axis in ("ty", "tx", "grp"))
    in_specs = (
        P(None, ("ty", "tx", "grp"), None, None),
        P(None, ("ty", "tx", "grp"), None),
        P(None, ("ty", "tx", "grp"), None),
        P(None, ("ty", "tx", "grp"), None),
        P(None, ("ty", "tx", "grp")),
        P("ty", ("tx", "grp")),
        P("ty", ("tx", "grp")),
        P(None, "ty", ("tx", "grp")),
        P(),
        P(None, None, ("ty", "grp"), "tx"),
    )
    out_specs = P(None, None, "ty", ("tx", "grp"))
    return jax.shard_map(
        functools.partial(per_device, sizes), mesh=mesh, in_specs=in_specs, out_specs=out_specs, check_vma=False
    )
```

```python
import functools

import jax
import jax.numpy as jnp
from jax import lax
from jax.experimental import pallas as pl
from jax.experimental.pallas import tpu as pltpu
from jax.sharding import PartitionSpec as P

F = 5
LEV = 8
VARS = 2
ICEV = 4
ROWS = 8
LANES = 128
DEPTH = 128
PROFS = 128
ITERS = 2
SUB = 2
SLOTS = 32
N_FORCED = VARS * LEV + (ICEV - VARS)
N_STATIC = LEV + 2
MESH = pl.DeviceIdType.MESH
F32 = jnp.float32
BF16 = jnp.bfloat16
NT = (((1,), (1,)), ((), ()))

FORCED = [(f, l) for f in range(VARS) for l in range(LEV)] + [(f, 0) for f in range(VARS, ICEV)]

L_LEVEL, L_WEIGHT, L_INNOV, L_TILE, L_CELL, L_LAND, L_HDIFF, L_VDIFF, L_ICE, L_COUPLING, L_OWN, L_BORDER = range(12)
N_LOCAL = 12
R_ROUTE, R_ICE, R_STAT_Y, R_STAT_X, R_STAT_YE, R_BORDER, R_BORDER_ICE, R_BORDER_LAND = range(8)
R_FORCED_Y, R_FORCED_YE, R_FORCED_RIGHT, R_FORCED_LEFT = range(8, 16, 2)
N_REMOTE = 16
GROUPS = 3
S_NEAR, S_BESIDE, S_DIAGONAL = GROUPS, GROUPS + 1, GROUPS + 2

RANK_ROWS = 4
RANKS = 4
MESSAGE = RANK_ROWS + 1


def iota(shape, axis):
    return lax.broadcasted_iota(jnp.int32, shape, axis)


def split(x):
    high = x.astype(BF16)
    low = (x - high.astype(F32)).astype(BF16)
    return high, low


def roll_lanes(x, shift):
    shift %= LANES
    return x if shift == 0 else pltpu.roll(x, shift, 1)


def dot_nt(a, b):
    return lax.dot_general(a, b, NT, preferred_element_type=F32)


def level_sums(weight, level, innovs):
    level_t = level.T
    out = []
    for innov in innovs:
        weighted_t = (weight * innov).T
        rows = [
            jnp.sum(jnp.where(level_t == l, weighted_t, 0.0), axis=0, keepdims=True) for l in range(LEV)
        ]
        out.append(jnp.concatenate(rows, axis=0))
    return out


def rank_in_tile(tile):
    named = (tile == iota((SLOTS, PROFS), 0)).astype(F32)
    before = (iota((PROFS, PROFS), 0) < iota((PROFS, PROFS), 1)).astype(F32).astype(BF16)
    counts = lax.dot_general(
        named.astype(BF16), before, (((1,), (0,)), ((), ())), preferred_element_type=F32
    )
    return named.astype(BF16), jnp.sum(named * counts, axis=0, keepdims=True).astype(jnp.int32)


def pack_messages(columns, tiles, cells):
    row = iota((8, PROFS), 0)
    zero = jnp.zeros((8, PROFS), F32)
    named, ranks, tops, rests, yx = [], [], [], [], []
    for w in range(ITERS):
        n, rank = rank_in_tile(tiles[w])
        named += [n, n]
        ranks.append(rank)
        top = [c.astype(BF16).astype(F32) for c in columns[w]]
        tops.append(top)
        rests.append([c - t for c, t in zip(columns[w], top)])
        cell = cells[w]
        yx.append(jnp.where(row % 2 == 0, (cell // LANES).astype(F32), (cell % LANES).astype(F32)))
    high = [[], []]
    low = [[], []]

    def add(w, top, rest):
        for u in range(ITERS):
            high[u].append(top if u == w else zero)
            low[u].append(rest if u == w else zero)

    for upper in range(RANK_ROWS):
        for w in range(ITERS):
            for v in range(VARS):
                for r in range(RANKS):
                    here = ranks[w] == upper * RANKS + r
                    add(w, jnp.where(here, tops[w][v], 0.0), jnp.where(here, rests[w][v], 0.0))
    for upper in range(RANK_ROWS):
        for w in range(ITERS):
            add(w, jnp.where(ranks[w] == upper * RANKS + row // 2, yx[w], 0.0), zero)
        add(0, zero, zero)
        add(0, zero, zero)
    values = jnp.concatenate(
        [jnp.concatenate(part[w], axis=0).astype(BF16) for w in range(ITERS) for part in (high, low)], axis=1
    )
    return dot_nt(jnp.concatenate(named, axis=1), values)


def gather_cells(received):
    got = jnp.concatenate([received(j) for j in range(RANK_ROWS)], axis=0).T
    cells = received(RANK_ROWS)
    where_ = jnp.concatenate([roll_lanes(cells, -32 * j) for j in range(RANK_ROWS)], axis=0).T
    top = got.astype(BF16).astype(F32)
    rest = got - top
    y_of_row = iota((ROWS, LANES), 0).astype(F32)
    x_of_row = iota((LANES, LANES), 0).astype(F32)
    for w in range(ITERS):
        left, right = [], []
        for r in range(RANKS):
            at = (w * RANKS + r) * 2
            y_here = where_[at : at + 1] == y_of_row
            x_here = (where_[at + 1 : at + 2] == x_of_row).astype(F32).astype(BF16)
            for part in (top, rest):
                blocks = []
                for v in range(VARS):
                    for l in range(LEV):
                        at = w * 64 + v * 32 + r * LEV + l
                        blocks.append(jnp.where(y_here, part[at : at + 1], 0.0))
                left.append(jnp.concatenate(blocks, axis=0).astype(BF16))
                right.append(x_here)
        yield dot_nt(jnp.concatenate(left, axis=1), jnp.concatenate(right, axis=1))


def gather_edges(received, firsts):
    got = jnp.concatenate([received(j) for j in range(RANK_ROWS)], axis=0).T
    cells = received(RANK_ROWS)
    where_ = jnp.concatenate([roll_lanes(cells, -32 * j) for j in range(RANK_ROWS)], axis=0).T
    top = got.astype(BF16).astype(F32)
    rest = got - top
    row = iota((ROWS, LANES), 0)
    y_of_row = row.astype(F32)
    zero = jnp.zeros((ROWS, LANES), F32)
    for w in range(ITERS):
        left, right = [], []
        for r in range(RANKS):
            at = (w * RANKS + r) * 2
            y_here = (where_[at : at + 1] == y_of_row).astype(F32)
            x_here = [where_[at + 1 : at + 2] == (first + row % 4).astype(F32) for first in firsts]
            for part in (top, rest):
                blocks = [[] for _ in firsts]
                for l in range(LEV):
                    at = w * 64 + r * LEV + l
                    both = jnp.where(row < 4, part[at : at + 1], part[at + 32 : at + 33])
                    for block, here in zip(blocks, x_here):
                        block += [jnp.where(here, both, 0.0), zero]
                left.append(y_here)
                right.append(jnp.concatenate(sum(blocks, []), axis=0).astype(BF16))
        sums = dot_nt(jnp.concatenate(left, axis=1).astype(BF16), jnp.concatenate(right, axis=1))
        yield [sums[:, i * LANES : (i + 1) * LANES] for i in range(len(firsts))]


def edge_ocean(ocean, first):
    lane = iota((ROWS, LANES), 1)
    out = jnp.where(lane < 4, roll_lanes(ocean, -first), 0.0)
    for width in (4, 8, 16, 32, 64):
        out = out + roll_lanes(out, width)
    return out


def edge_melt(melts, first):
    lane = iota((ROWS, LANES), 1)
    out = jnp.zeros((ROWS, LANES), F32)
    for f, melt in enumerate(melts):
        here = jnp.logical_and(lane >= 4 * f, lane < 4 * f + 4)
        out = jnp.where(here, roll_lanes(melt, 4 * f - first), out)
    return out


def pack_edges(items):
    lane = iota((ROWS, LANES), 1)
    last = jnp.zeros((ROWS, LANES), F32)
    first = jnp.zeros((ROWS, LANES), F32)
    for slot, level, rows in items:
        at = 16 * level + 4 * slot
        turned = roll_lanes(rows, at + 4)
        last = jnp.where(jnp.logical_and(lane >= at, lane < at + 4), turned, last)
        first = jnp.where(jnp.logical_and(lane >= at + 4, lane < at + 8), turned, first)
    return last, first


def strip(slot, from_left, own_last, own_first, from_right):
    group = iota((ROWS, LANES), 1) % 16
    low = jnp.where(group < 4, roll_lanes(from_left, -4 * slot), roll_lanes(own_first, -4 * slot))
    high = jnp.where(group < 12, roll_lanes(own_last, 8 - 4 * slot), roll_lanes(from_right, 8 - 4 * slot))
    return jnp.where(group < 8, low, high)


def strips(slots, received, own):
    upper = iota((ROWS, LANES), 0) < 4
    left_halo = jnp.where(upper, received[1], received[2])
    right_halo = jnp.where(upper, received[4], received[5])
    sides = ((received[0], received[3]), (left_halo, right_halo))
    return [
        tuple(strip(slot, sides[t][0], own[t][0], own[t][1], sides[t][1]) for t in range(2)) for slot in slots
    ]


def y_neighbours(pair):
    row = iota((ROWS, LANES), 0)
    a, b = pair
    next_a, next_b = pltpu.roll(a, ROWS - 1, 0), pltpu.roll(b, ROWS - 1, 0)
    prev_a, prev_b = pltpu.roll(a, 1, 0), pltpu.roll(b, 1, 0)
    plus = (jnp.where(row == ROWS - 1, next_b, next_a), jnp.where(row == ROWS - 1, next_a, next_b))
    minus = (jnp.where(row == 0, prev_b, prev_a), jnp.where(row == 0, prev_a, prev_b))
    return plus, minus


def edge_pair(one):
    group = iota((ROWS, LANES), 1) % 16
    return jnp.where(group == 13, roll_lanes(one, 10), one)


def x_neighbours(one, edges, level):
    lane = iota((ROWS, LANES), 1)
    halo = roll_lanes(edges, LANES - 1 - 12 - 16 * level)
    plus = jnp.where(lane == LANES - 1, halo, roll_lanes(one, -1))
    minus = jnp.where(lane == 0, halo, roll_lanes(one, 1))
    return plus, minus


def strip_x_neighbours(one):
    return roll_lanes(one, -1), roll_lanes(one, 1)


def weights_of(diff, ocean, x_pairs):
    (diff_n, ocean_n) = (y_neighbours(diff), y_neighbours(ocean))
    out = []
    for t in range(2):
        near = [(diff_n[0][t], ocean_n[0][t]), (diff_n[1][t], ocean_n[1][t])] + list(x_pairs[t])
        faces = [0.5 * (diff[t] + d) * ocean[t] * o for d, o in near]
        out.append((1.0 - (faces[0] + faces[1] + faces[2] + faces[3]), faces))
    return out


def lateral(one, near, weights):
    centre, faces = weights
    total = centre * one
    for face, value in zip(faces, near):
        total = total + face * value
    return total


def couple(diffused, coef, ocean):
    out = []
    for f in range(F):
        total = None
        for g in range(F):
            if diffused[g] is not None:
                term = coef[g][f] * diffused[g]
                total = term if total is None else total + term
        out.append(ocean * total)
    return out


def step_strips(old, weights, vertical, ocean, coef):
    lane = iota((ROWS, LANES), 1)
    diffused = [[None] * F, [None] * F]
    for f in range(F):
        if old[f] is None:
            continue
        plus, minus = y_neighbours(old[f])
        for t in range(2):
            one = old[f][t]
            x_plus, x_minus = strip_x_neighbours(one)
            below = jnp.where(lane < LANES - 16, roll_lanes(one, -16), 0.0)
            flux = vertical[t] * (below - one)
            above = jnp.where(lane < 16, 0.0, roll_lanes(flux, 16))
            diffused[t][f] = lateral(one, (plus[t], minus[t], x_plus, x_minus), weights[t]) + (flux - above)
    coupled = [couple(diffused[t], coef, ocean[t]) for t in range(2)]
    return [(coupled[0][f], coupled[1][f]) for f in range(F)]


def step_tile(read, write, live, edges, weights, vertical, ocean, coef, tiles):
    above = [[None] * F, [None] * F]
    for l in range(LEV):
        diffused = [[None] * F, [None] * F]
        for f in range(F):
            here = read(f, l) if (f, l) in live else None
            below = read(f, l + 1) if (f, l + 1) in live else None
            near = y_neighbours(here) if here is not None else None
            for t in range(tiles):
                flux = None
                if here is not None and below is not None:
                    flux = vertical(l, t) * (below[t] - here[t])
                elif here is not None:
                    flux = -(vertical(l, t) * here[t])
                elif below is not None:
                    flux = vertical(l, t) * below[t]
                total = None
                if here is not None:
                    x_plus, x_minus = x_neighbours(here[t], edges[f][t], l)
                    total = lateral(here[t], (near[0][t], near[1][t], x_plus, x_minus), weights[t])
                if flux is not None:
                    total = flux if total is None else total + flux
                if above[t][f] is not None:
                    total = -above[t][f] if total is None else total - above[t][f]
                above[t][f] = flux
                diffused[t][f] = total
        for t in range(tiles):
            for f, value in enumerate(couple(diffused[t], coef, ocean[t])):
                write(f, l, t, value)


def kernel(
    sizes,
    innov,
    weight,
    level,
    tile,
    cell,
    land,
    hdiff,
    vdiff,
    coupling,
    ice,
    out,
    innov_v,
    weight_v,
    level_v,
    tile_v,
    cell_v,
    land_v,
    coupling_v,
    ice_v,
    stat,
    stat_y,
    stat_e,
    stat_x,
    send,
    recv,
    forced,
    forced_y,
    forced_e,
    forced_x,
    stat_ye,
    forced_ye,
    border,
    border_edge,
    border_ice,
    border_land,
    border_e,
    state,
    local_sem,
    send_sem,
    recv_sem,
    enter_sem,
):
    n_ty, n_tx, n_grp = sizes
    ty, tx, grp = lax.axis_index("ty"), lax.axis_index("tx"), lax.axis_index("grp")
    blocks = n_tx * n_grp
    block = tx * n_grp + grp
    right, left = (block + 1) % blocks, (block + blocks - 1) % blocks
    down, up = (ty + 1) % n_ty, (ty + n_ty - 1) % n_ty

    def at(row, column):
        return (row, column // n_grp, column % n_grp)

    half = n_tx // 2
    z, side = tx % half, tx // half
    at_first = jnp.logical_and(z == 0, grp == 1)
    at_last = jnp.logical_and(z == half - 1, grp == 1)

    def fetch(src, dst, sem):
        copy = pltpu.make_async_copy(src, dst, local_sem.at[sem])
        copy.start()
        return copy

    def put(src, dst, sem, device):
        pltpu.make_async_remote_copy(
            src_ref=src,
            dst_ref=dst,
            send_sem=send_sem.at[sem],
            recv_sem=recv_sem.at[sem],
            device_id=device,
            device_id_type=MESH,
        ).start()

    def wait(ref, sems, sem):
        pltpu.make_async_copy(ref, ref, sems.at[sem]).wait()

    def signal(sem, device):
        pl.semaphore_signal(sem, inc=1, device_id=device, device_id_type=MESH)

    def peers(low, high, act):
        def one(i, carry):
            for half_of in range(2):
                act(i + half_of * half)
            return carry

        lax.fori_loop(low, high, one, 0)

    def turn_y(row):
        chip, chips = row // 2, n_ty // 2
        return 2 * jnp.where(chip < chips // 2, chip, chips + chips // 2 - 1 - chip) + 1 - row % 2

    partner = (ty, tx, 1 - grp)
    nearest = [
        (at(down, block), turn_y(down) > turn_y(ty)),
        (at(up, block), turn_y(up) > turn_y(ty)),
        (partner, grp == 0),
    ]
    bounds = [0, half // 4, half // 2, half]
    group = jnp.where(z >= bounds[1], 1, 0) + jnp.where(z >= bounds[2], 1, 0)

    if n_tx < SLOTS:
        recv[...] = jnp.zeros(recv.shape, F32)
        border[...] = jnp.zeros(border.shape, F32)

    barrier = pltpu.get_barrier_semaphore()
    for device, after in nearest:
        pl.when(after)(functools.partial(signal, barrier, device))

    @pl.when(side == 0)
    def _():
        signal(barrier, (ty, tx + half, grp))

    def greet(peer):
        signal(barrier, (ty, peer, grp))

    middle = jnp.maximum(z + 1, bounds[GROUPS - 1])
    peers(middle, half, greet)

    at_border = jnp.logical_and(z == 0, grp == 0)

    @pl.when(at_border)
    def _():
        signal(barrier, (ty, (tx + n_tx - 1) % n_tx, 1))

    @pl.when(at_first)
    def _():
        signal(barrier, (ty, (tx + n_tx - 1) % n_tx, 0))

    earlier = 2 * z + side + jnp.where(z == half - 1, 1, 0)
    later_near = 0
    for _, after in nearest:
        earlier = earlier + jnp.where(after, 0, 1)
        later_near = later_near + jnp.where(after, 1, 0)

    def await_signals(sem, count):
        @pl.when(count > 0)
        def _():
            pl.semaphore_wait(sem, count)

    loads = [
        fetch(level, level_v, L_LEVEL),
        fetch(weight, weight_v, L_WEIGHT),
        fetch(innov, innov_v, L_INNOV),
        fetch(tile, tile_v, L_TILE),
        fetch(cell, cell_v, L_CELL),
    ]
    ice_here = ice.at[:, :, :, pl.ds(pl.multiple_of(grp * LANES, LANES), LANES)]
    ice_there = ice.at[:, :, :, pl.ds(pl.multiple_of((1 - grp) * LANES, LANES), LANES)]
    ice_last = ice.at[:, :, :, pl.ds((n_grp - 1) * LANES, LANES)]
    static_loads = [
        fetch(land, land_v, L_LAND),
        fetch(hdiff, stat.at[LEV], L_HDIFF),
        fetch(vdiff, stat.at[pl.ds(0, LEV)], L_VDIFF),
        fetch(ice_here, ice_v.at[grp], L_ICE),
        fetch(coupling, coupling_v, L_COUPLING),
    ]

    peers(z + 1, middle, greet)

    for load in loads:
        load.wait()
    columns = [
        level_sums(
            weight_v[w],
            level_v[w],
            [innov_v[pl.ds(w * PROFS * VARS + v, PROFS, stride=VARS), :] for v in range(VARS)],
        )
        for w in range(ITERS)
    ]
    messages = pack_messages(
        columns, [tile_v[pl.ds(w, 1), :] for w in range(ITERS)], [cell_v[pl.ds(w, 1), :] for w in range(ITERS)]
    )
    for j in range(MESSAGE):
        send[:, j, :] = messages[:, j * LANES : (j + 1) * LANES]

    await_signals(barrier, earlier)
    for load in static_loads:
        load.wait()
    ocean_tile = land_v[...].astype(F32)
    stat[LEV + 1] = ocean_tile

    @pl.when(z == half - 1)
    def _():
        put(ice_last, border_ice.at[grp], R_BORDER_ICE, (ty, (tx + 1) % n_tx, 1))

    @pl.when(at_last)
    def _():
        put(stat.at[LEV + 1], border_land, R_BORDER_LAND, (ty, (tx + 1) % n_tx, 1))

    for device, after in nearest:
        pl.when(jnp.logical_not(after))(functools.partial(signal, enter_sem.at[S_NEAR], device))

    @pl.when(jnp.logical_and(grp == 1, z > 0))
    def _():
        signal(enter_sem.at[S_BESIDE], (ty, tx - 1, 1))

    def route(peer):
        put(send.at[peer], recv.at[tx], R_ROUTE, (ty, peer, grp))

    def route_border(first_tx):
        put(send.at[(first_tx + n_tx - 1) % n_tx], border.at[tx], R_BORDER, (ty, first_tx, 1))

    @pl.when(jnp.logical_and(grp == 1, z > 0))
    def _():
        route_border(0)
        route_border(half)

    @pl.when(jnp.logical_and(at_first, side == 1))
    def _():
        route_border(0)

    peers(0, z, route)

    @pl.when(side == 1)
    def _():
        route(tx - half)

    peers(0, z, lambda peer: signal(enter_sem.at[group], (ty, peer, grp)))

    @pl.when(side == 1)
    def _():
        signal(enter_sem.at[group], (ty, tx - half, grp))

    own = fetch(send.at[tx], recv.at[tx], L_OWN)

    @pl.when(at_first)
    def _():
        pltpu.make_async_copy(
            send.at[(tx + n_tx - 1) % n_tx], border.at[tx], local_sem.at[L_BORDER]
        ).start()

    def static_items(ref):
        items = [(0, l, ref[l]) for l in range(LEV)]
        return items + [(1 + j, l, ref[LEV + j]) for j in range(2) for l in range(LEV)]

    last, first = pack_edges(static_items(stat))
    stat_e[0] = last
    stat_e[1] = first

    def route_later(g):
        low, high = bounds[g], bounds[g + 1]
        start = jnp.maximum(z + 1, low)
        twin = jnp.logical_and(side == 0, group == g)
        await_signals(enter_sem.at[g], 2 * jnp.maximum(high - start, 0) + jnp.where(twin, 1, 0))
        peers(start, high, route)

        @pl.when(twin)
        def _():
            route(tx + half)
            pl.when(at_first)(functools.partial(route_border, half))

    for g in range(GROUPS - 1):
        route_later(g)
    await_signals(enter_sem.at[S_NEAR], later_near)
    for r in (up, down):
        signal(enter_sem.at[S_DIAGONAL], at(r, block))
    put(ice_there, ice_v.at[grp], R_ICE, partner)

    def tell():
        signal(enter_sem.at[S_BESIDE], (ty, (tx + 1) % n_tx, 0))

    soon = jnp.logical_or(z + 1 < bounds[GROUPS - 1], z == half - 1)
    pl.when(jnp.logical_and(grp == 0, soon))(tell)
    route_later(GROUPS - 1)
    pl.when(jnp.logical_and(grp == 0, jnp.logical_not(soon)))(tell)
    def exchange_y(rows, rows_y, sem):
        for r, part in ((up, pl.ds(0, 4)), (down, pl.ds(4, 4))):
            whole_ = (slice(None),) * (len(rows.shape) - 2)
            put(rows.at[*whole_, part], rows_y.at[*whole_, part], sem, at(r, block))

    slots = ((2, down, pl.ds(4, 4)), (1, up, pl.ds(0, 4)), (0, ty, pl.ds(0, ROWS)))

    def exchange_x(edge, column, rows, rows_x, sem):
        for slot, r, part in slots:
            put(rows.at[edge, part], rows_x.at[edge * 3 + slot, part], sem, at(r, column))

    beside = jnp.where(grp == 0, left, right)

    def meet_beside():
        await_signals(enter_sem.at[S_BESIDE], jnp.where(jnp.logical_or(grp == 0, z < half - 1), 1, 0))
        for r in (up, down):
            signal(enter_sem.at[S_DIAGONAL + 1], at(r, block))
        pl.semaphore_wait(enter_sem.at[S_DIAGONAL + 1], 2)
        exchange_x(1 - grp, beside, stat_e, stat_x, R_STAT_X)

    def force_beside(w):
        @pl.when(jnp.logical_not(at_last))
        def _():
            exchange_x(1 - grp, beside, forced_e.at[w], forced_x.at[w], R_FORCED_RIGHT + 2 * (1 - grp) + w)

    pl.semaphore_wait(enter_sem.at[S_DIAGONAL], 2)
    exchange_y(stat, stat_y, R_STAT_Y)
    exchange_y(stat_e, stat_ye, R_STAT_YE)
    exchange_x(grp, tx * n_grp + 1 - grp, stat_e, stat_x, R_STAT_X)
    pl.when(jnp.logical_not(at_border))(meet_beside)

    def melts_of(ref, w):
        return [jnp.concatenate([ref[0, w, f], ref[1, w, f]], axis=0) for f in range(ICEV)]

    last_cols, first_cols = LANES - 4, 0
    wait(ice_v.at[0], recv_sem, R_ICE)
    melts = [melts_of(ice_v, w) for w in range(ITERS)]
    oceans_e = [edge_ocean(ocean_tile, first) for first in (last_cols, first_cols)]
    melts_e = [[edge_melt(melts[w], first) for first in (last_cols, first_cols)] for w in range(ITERS)]

    @pl.when(at_first)
    def _():
        wait(border_land, recv_sem, R_BORDER_LAND)
        wait(border_ice, recv_sem, R_BORDER_ICE)
        border_edge[0] = edge_ocean(border_land[...], last_cols)
        for w in range(ITERS):
            border_edge[1 + w] = edge_melt(melts_of(border_ice, w), last_cols)

    own.wait()
    wait(recv.at[pl.ds(0, n_tx - 1)], recv_sem, R_ROUTE)
    window_edges = gather_edges(lambda j: recv[:, j, :], (last_cols, first_cols))
    window_sums = gather_cells(lambda j: recv[:, j, :])
    for w in range(ITERS):
        sums = next(window_edges)
        last, first = [oceans_e[i] * (sums[i] + melts_e[w][i]) for i in range(2)]
        forced_e[w, 0] = last
        forced_e[w, 1] = roll_lanes(first, 4)
        pl.when(jnp.logical_not(at_border))(functools.partial(force_beside, w))
        exchange_x(grp, tx * n_grp + 1 - grp, forced_e.at[w], forced_x.at[w], R_FORCED_RIGHT + 2 * grp + w)
        exchange_y(forced_e.at[w], forced_ye.at[w], R_FORCED_YE + w)
        if w == 0:

            @pl.when(at_first)
            def _():
                wait(border.at[tx], local_sem, L_BORDER)
                wait(border.at[pl.ds(0, n_tx - 1)], recv_sem, R_BORDER)
                border_sums = gather_edges(lambda j: border[:, j, :], (last_cols,))
                for u in range(ITERS):
                    border_e[u] = border_edge[0] * (next(border_sums)[0] + border_edge[1 + u])
                    for slot, r, part in slots:
                        put(border_e.at[u, part], forced_x.at[u, slot, part], R_FORCED_RIGHT + u, (r, tx, 0))

        sums = next(window_sums)
        for i, (f, l) in enumerate(FORCED):
            value = sums[i * ROWS : (i + 1) * ROWS] if f < VARS else None
            if l == 0:
                value = melts[w][f] if value is None else value + melts[w][f]
            forced[w * N_FORCED + i] = ocean_tile * value
        mine = pl.ds(w * N_FORCED, N_FORCED)
        exchange_y(forced.at[mine], forced_y.at[mine], R_FORCED_Y + w)

    @pl.when(at_border)
    def _():
        meet_beside()
        for w in range(ITERS):
            force_beside(w)

    wait(stat_y, recv_sem, R_STAT_Y)
    wait(stat_ye, recv_sem, R_STAT_YE)
    wait(stat_x.at[pl.ds(0, 4)], recv_sem, R_STAT_X)
    own_edges = ((stat_e[0], stat_e[1]), (stat_ye[0], stat_ye[1]))
    vertical_s, diff_s, ocean_s = strips((0, 1, 2), [stat_x[i] for i in range(6)], own_edges)
    diff = (stat[LEV], stat_y[LEV])
    ocean = (stat[LEV + 1], stat_y[LEV + 1])
    x_pairs, x_pairs_s = [], []
    for t in range(2):
        d = x_neighbours(diff[t], edge_pair(diff_s[t]), 0)
        o = x_neighbours(ocean[t], edge_pair(ocean_s[t]), 0)
        x_pairs.append(((d[0], o[0]), (d[1], o[1])))
        d, o = strip_x_neighbours(diff_s[t]), strip_x_neighbours(ocean_s[t])
        x_pairs_s.append(((d[0], o[0]), (d[1], o[1])))
    weights = weights_of(diff, ocean, x_pairs)
    weights_s = weights_of(diff_s, ocean_s, x_pairs_s)
    coef = [
        [
            jnp.broadcast_to(coupling_v[g : g + 1, f : f + 1], (ROWS, LANES)) + (1.0 if f == g else 0.0)
            for f in range(F)
        ]
        for g in range(F)
    ]

    def vertical(l, t):
        return stat[l] if t == 0 else stat_y[l]

    def forced_strips(w):
        wait(forced_y.at[pl.ds(w * N_FORCED, N_FORCED)], recv_sem, R_FORCED_Y + w)
        wait(forced_ye.at[w], recv_sem, R_FORCED_YE + w)
        wait(forced_x.at[w, pl.ds(0, 2)], recv_sem, R_FORCED_RIGHT + w)
        wait(forced_x.at[w, pl.ds(3, 2)], recv_sem, R_FORCED_LEFT + w)
        own_edges = ((forced_e[w, 0], forced_e[w, 1]), (forced_ye[w, 0], forced_ye[w, 1]))
        return strips(range(ICEV), [forced_x[w, i] for i in range(6)], own_edges)

    index = {item: i for i, item in enumerate(FORCED)}
    whole = {(f, l) for f in range(F) for l in range(LEV)}
    packed = forced_strips(0) + [None]

    def read_forced(f, l):
        return forced[index[f, l]], forced_y[index[f, l]]

    def reader(slot):
        return lambda f, l: (state[slot, 0, f * LEV + l], state[slot, 1, f * LEV + l])

    def writer(slot):
        def write(f, l, t, value):
            state[slot, t, f * LEV + l] = value

        return write

    def write_out(f, l, t, value):
        out[f, l] = value

    n_steps = ITERS * SUB
    for step in range(n_steps):
        end = step == n_steps - 1
        edges = [None if p is None else (edge_pair(p[0]), edge_pair(p[1])) for p in packed]
        step_tile(
            read_forced if step == 0 else reader(step % 2),
            write_out if end else writer((step + 1) % 2),
            set(FORCED) if step == 0 else whole,
            edges,
            weights,
            vertical,
            ocean,
            coef,
            1 if end else 2,
        )
        if not end:
            packed = step_strips(packed, weights_s, vertical_s, ocean_s, coef)
        if step == SUB - 1:
            slot = (step + 1) % 2
            added = forced_strips(1)
            for f in range(ICEV):
                packed[f] = tuple(packed[f][t] + added[f][t] for t in range(2))
            for i, (f, l) in enumerate(FORCED):
                state[slot, 0, f * LEV + l] += forced[N_FORCED + i]
                state[slot, 1, f * LEV + l] += forced_y[N_FORCED + i]

    wait(send.at[pl.ds(0, n_tx - 1)], send_sem, R_ROUTE)
    wait(ice_v.at[0], send_sem, R_ICE)
    wait(stat, send_sem, R_STAT_Y)
    wait(stat_ye, send_sem, R_STAT_YE)
    wait(stat_x.at[pl.ds(0, 4)], send_sem, R_STAT_X)
    for w in range(ITERS):
        wait(forced.at[pl.ds(w * N_FORCED, N_FORCED)], send_sem, R_FORCED_Y + w)
        wait(forced_ye.at[w], send_sem, R_FORCED_YE + w)
        wait(forced_x.at[w, pl.ds(0, 2)], send_sem, R_FORCED_LEFT + w)

        @pl.when(jnp.logical_not(at_last))
        def _():
            wait(forced_x.at[w, pl.ds(0, 2)], send_sem, R_FORCED_RIGHT + w)

        @pl.when(at_first)
        def _():
            wait(forced_x.at[w, pl.ds(0, 2)], send_sem, R_FORCED_RIGHT + w)

    @pl.when(grp == 1)
    def _():
        wait(send.at[0], send_sem, R_BORDER)

        @pl.when(z > 0)
        def _():
            wait(send.at[0], send_sem, R_BORDER)

    @pl.when(z == half - 1)
    def _():
        wait(border_ice.at[0], send_sem, R_BORDER_ICE)

    @pl.when(at_last)
    def _():
        wait(border_land, send_sem, R_BORDER_LAND)


def per_device(sizes, innov, weight, level, tile, cell, land, hdiff, vdiff, coupling, ice):
    scratch = [
        pltpu.VMEM((ITERS * PROFS * VARS, DEPTH), F32),
        pltpu.VMEM((ITERS, PROFS, DEPTH), F32),
        pltpu.VMEM((ITERS, PROFS, DEPTH), jnp.int32),
        pltpu.VMEM((ITERS, PROFS), jnp.int32),
        pltpu.VMEM((ITERS, PROFS), jnp.int32),
        pltpu.VMEM((ROWS, LANES), jnp.int32),
        pltpu.VMEM((F, F), F32),
        pltpu.VMEM((2, ITERS, ICEV, 4, LANES), F32),
        pltpu.VMEM((N_STATIC, ROWS, LANES), F32),
        pltpu.VMEM((N_STATIC, ROWS, LANES), F32),
        pltpu.VMEM((2, ROWS, LANES), F32),
        pltpu.VMEM((6, ROWS, LANES), F32),
        pltpu.VMEM((SLOTS, MESSAGE, LANES), F32),
        pltpu.VMEM((SLOTS, MESSAGE, LANES), F32),
        pltpu.VMEM((ITERS * N_FORCED, ROWS, LANES), F32),
        pltpu.VMEM((ITERS * N_FORCED, ROWS, LANES), F32),
        pltpu.VMEM((ITERS, 2, ROWS, LANES), F32),
        pltpu.VMEM((ITERS, 6, ROWS, LANES), F32),
        pltpu.VMEM((2, ROWS, LANES), F32),
        pltpu.VMEM((ITERS, 2, ROWS, LANES), F32),
        pltpu.VMEM((SLOTS, MESSAGE, LANES), F32),
        pltpu.VMEM((1 + ITERS, ROWS, LANES), F32),
        pltpu.VMEM((2, ITERS, ICEV, 4, LANES), F32),
        pltpu.VMEM((ROWS, LANES), F32),
        pltpu.VMEM((ITERS, ROWS, LANES), F32),
        pltpu.VMEM((2, 2, F * LEV, ROWS, LANES), F32),
        pltpu.SemaphoreType.DMA((N_LOCAL,)),
        pltpu.SemaphoreType.DMA((N_REMOTE,)),
        pltpu.SemaphoreType.DMA((N_REMOTE,)),
        pltpu.SemaphoreType.REGULAR((GROUPS + 4,)),
    ]
    operands = (
        innov.reshape(ITERS * PROFS * VARS, DEPTH),
        weight,
        level,
        tile.reshape(ITERS, PROFS),
        cell,
        land,
        hdiff,
        vdiff,
        coupling,
        ice,
    )
    anywhere = pl.BlockSpec(memory_space=pltpu.HBM)
    return pl.pallas_call(
        functools.partial(kernel, sizes),
        out_shape=jax.ShapeDtypeStruct((F, LEV, ROWS, LANES), F32),
        in_specs=[anywhere] * len(operands),
        out_specs=pl.BlockSpec(memory_space=pltpu.VMEM),
        scratch_shapes=scratch,
        compiler_params=pltpu.CompilerParams(
            collective_id=0, has_side_effects=True, vmem_limit_bytes=16 * 1024 * 1024
        ),
    )(*(pltpu.with_memory_space_constraint(operand, pltpu.HBM) for operand in operands))


def solution(mesh):
    sizes = tuple(mesh.shape[axis] for axis in ("ty", "tx", "grp"))
    in_specs = (
        P(None, ("ty", "tx", "grp"), None, None),
        P(None, ("ty", "tx", "grp"), None),
        P(None, ("ty", "tx", "grp"), None),
        P(None, ("ty", "tx", "grp"), None),
        P(None, ("ty", "tx", "grp")),
        P("ty", ("tx", "grp")),
        P("ty", ("tx", "grp")),
        P(None, "ty", ("tx", "grp")),
        P(),
        P(None, None, ("ty", "grp"), "tx"),
    )
    out_specs = P(None, None, "ty", ("tx", "grp"))
    return jax.shard_map(
        functools.partial(per_device, sizes), mesh=mesh, in_specs=in_specs, out_specs=out_specs, check_vma=False
    )
```
